128 devices in a mesh: fsdp: 4 (over y_lo, core), sp: 8 (over y_hi, x), tp: 4 (over z).
Axes of the slice: x: 4, y: 4 (y_hi: 2, y_lo: 2; y = y_hi * 2 + y_lo), z: 4, core: 2. Of those that a mesh axis runs over, the one named last changes fastest.
Arguments:
- tokens: bfloat16 [8, 2048, 2048], P('fsdp', 'sp'), may hold values from -6 to 6
- ln_gain: bfloat16 [2048], replicated, may hold values from 0.5 to 1.5
- ln_bias: bfloat16 [2048], replicated, may hold values from -1.25 to 1.25
- w_qkv: bfloat16 [2048, 3, 2048], P(('fsdp', 'sp'), None, 'tp'), may hold values from -0.1875 to 0.1875
- b_qkv: bfloat16 [3, 2048], P(None, 'tp'), may hold values from -1.75 to 1.75
- w_dense: bfloat16 [2048, 2048], P('tp', ('fsdp', 'sp')), may hold values from -1 to 1
- b_dense: bfloat16 [2048], replicated, may hold values from -3 to 3
- w_fc1: bfloat16 [2048, 8192], P(('fsdp', 'sp'), 'tp'), may hold values from -0.125 to 0.125
- b_fc1: bfloat16 [8192], P('tp'), may hold values from -1.75 to 1.75
- w_fc2: bfloat16 [8192, 2048], P('tp', ('fsdp', 'sp')), may hold values from -0.09375 to 0.09375
- b_fc2: bfloat16 [2048], replicated, may hold values from -3 to 3
- cotangent: bfloat16 [8, 2048, 2048], P('fsdp', 'sp'), may hold values from -6 to 6
Outputs:
- mixed_out: bfloat16 [8, 2048, 2048], P('fsdp', 'sp')
- grad_tokens: bfloat16 [8, 2048, 2048], P('fsdp', 'sp')
- grad_ln_gain: float32 [2048], replicated
- grad_ln_bias: float32 [2048], replicated
- grad_w_qkv: float32 [2048, 3, 2048], P(('fsdp', 'sp'), None, 'tp')
- grad_b_qkv: float32 [3, 2048], P(None, 'tp')
- grad_w_dense: float32 [2048, 2048], P('tp', ('fsdp', 'sp'))
- grad_b_dense: float32 [2048], replicated
- grad_w_fc1: float32 [2048, 8192], P(('fsdp', 'sp'), 'tp')
- grad_b_fc1: float32 [8192], P('tp')
- grad_w_fc2: float32 [8192, 2048], P('tp', ('fsdp', 'sp'))
- grad_b_fc2: float32 [2048], replicated
The draws below stay inside these ranges and needn't reach their ends.
All inputs are finite; a program needn't handle non-finite values.
Results may differ from the reference program's by a relative error of at most 0.023.
Values may be sent and summed in bfloat16 or wider, within the bound.
A program may use at most 192 MiB of HBM per device.

```python
import math
import jax
import jax.numpy as jnp
from jax import lax

D = 2048
HEADS = 32
HDIM = 64
ROT = 32
FF = 8192
SEQ_LEN = 2048
SEQS = 8


def block_levels(key, extent, shards, low, high):
    gain = 1.0
    for dim, parts in shards:
        steps = jax.random.uniform(jax.random.fold_in(jax.random.fold_in(key, 6), dim), (parts,), jnp.float32, low / len(shards), high / len(shards))
        gain = gain * jnp.repeat(jnp.exp(steps), extent[dim] // parts).reshape((-1,) + (1,) * (len(extent) - 1 - dim))
    return gain


def noise(own_key, dims, deviation, limit, cuts=(), kind=jnp.bfloat16):
    factor_of = block_levels(own_key, dims, cuts, -0.22, 0.18) if cuts else 1.0
    drawn = jax.random.normal(own_key, dims, jnp.float32) * deviation * factor_of
    return jnp.minimum(jnp.maximum(drawn, -limit), limit).astype(kind)


def setup_inputs(seed: int = 0) -> dict:
    key_of = jax.random.split(jax.random.key(seed), 13)
    return {
        "tokens": noise(key_of[0], (SEQS, SEQ_LEN, D), 1.0, 6.0, ((0, 4), (1, 8))),
        "ln_gain": jnp.clip(1.0 + 0.1 * jax.random.normal(key_of[1], (D,), jnp.float32), 0.5, 1.5).astype(jnp.bfloat16),
        "ln_bias": noise(key_of[2], (D,), 0.2, 1.25),
        "w_qkv": noise(key_of[3], (D, 3, D), (D // 2) ** -0.5, 0.1875, ((0, 32), (2, 4))),
        "b_qkv": noise(key_of[4], (3, D), 0.3, 1.75, ((1, 4),)),
        "w_dense": noise(key_of[5], (D, D), (D // 64) ** -0.5, 1.0, ((0, 4), (1, 32))),
        "b_dense": noise(key_of[6], (D,), 0.5, 3.0),
        "w_fc1": noise(key_of[7], (D, FF), D ** -0.5, 0.125, ((0, 32), (1, 4))),
        "b_fc1": noise(key_of[8], (FF,), 0.3, 1.75, ((0, 4),)),
        "w_fc2": noise(key_of[9], (FF, D), (FF // 2) ** -0.5, 0.09375, ((0, 4), (1, 32))),
        "b_fc2": noise(key_of[10], (D,), 0.5, 3.0),
        "cotangent": noise(key_of[11], (SEQS, SEQ_LEN, D), 1.0, 6.0, ((0, 4), (1, 8))),
    }


@jax.custom_vjp
def low(v):
    return lax.optimization_barrier(v.astype(jnp.bfloat16)).astype(jnp.float32)

@jax.custom_vjp
def low_back(v):
    return v

def low_keep(v):
    return (low(v), None)

def low_pass(kept, grad):
    return (grad,)

def back_keep(v):
    return (v, None)

def back_low(kept, grad):
    return (low(grad),)
low.defvjp(low_keep, low_pass)
low_back.defvjp(back_keep, back_low)

def mult(left, right):
    return jnp.dot(left, right, precision=lax.Precision.HIGHEST)

def rotate(part, cosine, sine):
    half = ROT // 2
    first_half = part[..., :half]
    second_half = part[..., half:ROT]
    remain = part[..., ROT:]
    return jnp.concatenate([first_half * cosine - second_half * sine, second_half * cosine + first_half * sine, remain], axis=-1)

def one_head(pieces):
    query, key_part, value = pieces
    scores = low_back(mult(query, key_part.T) * HDIM ** (-0.5))
    places = jnp.arange(SEQ_LEN, dtype=jnp.int32)
    causal = places[:, None] >= places[None, :]
    scores = jnp.where(causal, scores, -1e+30)
    row_top = lax.optimization_barrier(jnp.max(scores, axis=-1, keepdims=True))
    weights = jnp.exp(scores - row_top)
    probs = weights / lax.optimization_barrier(jnp.sum(weights, axis=-1, keepdims=True))
    return mult(low(probs), value)

def forward(inputs, ln_gain, ln_bias, w_qkv, b_qkv, w_dense, b_dense, w_fc1, b_fc1, w_fc2, b_fc2):
    average = lax.optimization_barrier(jnp.mean(inputs, axis=-1, keepdims=True))
    centered = inputs - average
    spread = lax.optimization_barrier(jnp.mean(centered * centered, axis=-1, keepdims=True))
    normed = centered * lax.rsqrt(spread + 1e-05) * ln_gain + ln_bias
    hidden = low(normed)
    projected = low_back(mult(hidden, w_qkv.reshape(D, 3 * D)) + b_qkv.reshape(3 * D))
    projected = projected.reshape(SEQ_LEN, 3, HEADS, HDIM)
    places = jnp.arange(SEQ_LEN, dtype=jnp.float32)
    freqs = jnp.exp(jnp.arange(ROT // 2, dtype=jnp.float32) * (-2.0 * math.log(10000.0) / ROT))
    angle = places[:, None, None] * freqs[None, None, :]
    cosine = jnp.cos(angle)
    sine = jnp.sin(angle)
    query = low_back(low(rotate(projected[:, 0], cosine, sine)))
    key_part = low_back(low(rotate(projected[:, 1], cosine, sine)))
    value = low(projected[:, 2])
    heads_out = lax.map(jax.checkpoint(one_head), (query.transpose(1, 0, 2), key_part.transpose(1, 0, 2), value.transpose(1, 0, 2)))
    attended = low_back(low(heads_out.transpose(1, 0, 2).reshape(SEQ_LEN, D)))
    attn_out = mult(attended, w_dense) + b_dense
    inner = low_back(mult(hidden, w_fc1) + b_fc1)
    active = low(jax.nn.gelu(inner, approximate=True))
    mlp_out = mult(active, w_fc2) + b_fc2
    return inputs + attn_out + mlp_out

def reference(tokens, ln_gain, ln_bias, w_qkv, b_qkv, w_dense, b_dense, w_fc1, b_fc1, w_fc2, b_fc2, cotangent):
    params = tuple((item.astype(jnp.float32) for item in (ln_gain, ln_bias, w_qkv, b_qkv, w_dense, b_dense, w_fc1, b_fc1, w_fc2, b_fc2)))

    def per_sequence(totals, pair):
        seq_rows, seq_grad = pair
        result, pull = jax.vjp(forward, seq_rows.astype(jnp.float32), *params)
        grads = pull(seq_grad.astype(jnp.float32))
        summed = tuple((left + right for left, right in zip(totals, grads[1:])))
        return (summed, (result.astype(jnp.bfloat16), grads[0].astype(jnp.bfloat16)))
    zeros = tuple((jnp.zeros(item.shape, jnp.float32) for item in params))
    totals, outputs = lax.scan(per_sequence, zeros, (tokens, cotangent))
    mixed_out, grad_tokens = outputs
    return (mixed_out, grad_tokens, totals[0], totals[1], totals[2], totals[3], totals[4], totals[5], totals[6], totals[7], totals[8], totals[9])
```

```python
import functools
import math

import jax
import jax.numpy as jnp
from jax import lax
from jax.experimental import pallas as pl
from jax.experimental.pallas import tpu as pltpu
from jax.sharding import PartitionSpec as P

MESH = pl.DeviceIdType.MESH
F32 = jnp.float32
BF = jnp.bfloat16
HDIM = 64
ROT = 32
TQ = 512
LOG2E = 1.4426950408889634
MIB = 2**20


def dot_nt(a, b):
    return lax.dot_general(a, b, (((1,), (1,)), ((), ())), preferred_element_type=F32)


def dot_nn(a, b):
    return lax.dot_general(a, b, (((1,), (0,)), ((), ())), preferred_element_type=F32)


class Scratch:
    def __init__(self, names, refs):
        for name, ref in zip(names, refs):
            setattr(self, name, ref)


class Place:
    def __init__(self):
        f, s, t = (lax.axis_index(a) for a in ("fsdp", "sp", "tp"))
        self.f, self.s = f, s
        self.x, self.y, self.c, self.z = s % 4, (s // 4) * 2 + f // 2, f % 2, t
        self.a1 = self.x * (1 - self.c) + self.y * self.c
        self.a2 = self.y * (1 - self.c) + self.x * self.c

    def xy(self, d1, d2):
        p1, p2, c = (self.a1 + d1 + 4) % 4, (self.a2 + d2 + 4) % 4, self.c
        return p1 * (1 - c) + p2 * c, p2 * (1 - c) + p1 * c

    def dev(self, x, y, c, z):
        return ((y % 2) * 2 + c, (y // 2) * 4 + x, z)

    def peer(self, d1, d2):
        x, y = self.xy(d1, d2)
        return self.dev(x, y, self.c, self.z)

    def sibling(self):
        return self.dev(self.x, self.y, 1 - self.c, self.z)

    def blk(self, d1, d2):
        x, y = self.xy(d1, d2)
        return ((y % 2) * 2 + self.c) * 8 + (y // 2) * 4 + x

    def zpeer(self, d):
        return self.dev(self.x, self.y, self.c, (self.z + d + 4) % 4)

    def sp_peer(self, k):
        return (self.f, (self.s + k) % 8, self.z)


def barrier(devices):
    sem = pltpu.get_barrier_semaphore()
    for d in devices:
        pl.semaphore_signal(sem, inc=1, device_id=d, device_id_type=MESH)
    pl.semaphore_wait(sem, len(devices))


def remote(src, dst, send, recv, device):
    pltpu.make_async_remote_copy(
        src_ref=src, dst_ref=dst, send_sem=send, recv_sem=recv, device_id=device, device_id_type=MESH
    ).start()


def wait_bytes(ref, sem):
    pltpu.make_async_copy(ref, ref, sem).wait()


STEP = (0, -1, 1, 2)


class Gather:
    def __init__(self, p, shard, w, send, recv, local):
        self.p, self.shard, self.w, self.send, self.recv, self.local = p, shard, w, send, recv, local

    def push(self, b, sem, device, half=None, src=None):
        dst = self.w.at[b] if half is None else self.w.at[b, pl.ds(32 * half, 32)]
        remote(dst if src is None else src, dst, self.send, self.recv.at[sem], device)

    def arrive(self, b, sem):
        wait_bytes(self.w.at[b], self.recv.at[sem])

    def start(self):
        p, s = self.p, self.shard
        own = p.blk(0, 0)
        for sem, device in ((0, p.peer(1, 0)), (1, p.peer(-1, 0)), (3, p.peer(0, 1)), (7, p.peer(0, -1)), (15, p.sibling())):
            self.push(own, sem, device, src=s)
        pltpu.make_async_copy(s, self.w.at[own], self.local).start()

    def second(self, j):
        p = self.p
        b = p.blk(STEP[j], 0)
        self.push(b, 3 + j, p.peer(0, 1))
        self.push(b, 7 + j, p.peer(0, -1))
        self.push(b, 15, p.sibling())

    def first_low(self):
        p = self.p
        b = p.blk(-1, 0)
        self.arrive(b, 0)
        self.push(b, 2, p.peer(1, 0), half=0)
        self.second(1)

    def first_high(self):
        p = self.p
        b = p.blk(1, 0)
        self.arrive(b, 1)
        self.push(b, 2, p.peer(-1, 0), half=1)
        self.second(2)

    def first_far(self):
        self.arrive(self.p.blk(2, 0), 2)
        self.second(3)

    def low(self, j):
        p = self.p
        b = p.blk(STEP[j], -1)
        self.arrive(b, 3 + j)
        self.push(b, 11 + j, p.peer(0, 1), half=0)
        self.push(b, 15, p.sibling())

    def high(self, j):
        p = self.p
        b = p.blk(STEP[j], 1)
        self.arrive(b, 7 + j)
        self.push(b, 11 + j, p.peer(0, -1), half=1)
        self.push(b, 15, p.sibling())

    def far(self, j):
        b = self.p.blk(STEP[j], 2)
        self.arrive(b, 11 + j)
        self.push(b, 15, self.p.sibling())

    def end(self):
        wait_bytes(self.w.at[pl.ds(0, 16)], self.recv.at[15])
        own = self.p.blk(0, 0)
        pltpu.make_async_copy(self.shard, self.w.at[own], self.local).wait()

    def drain(self):
        wait_bytes(self.w.at[pl.ds(0, 31)], self.send)

    def ticks(self):
        part = functools.partial
        return [
            self.first_low, self.first_high, part(self.low, 0), part(self.high, 0), self.first_far,
            part(self.low, 1), part(self.high, 1), part(self.far, 0), part(self.low, 2), part(self.high, 2), part(self.far, 1),
            part(self.low, 3), part(self.high, 3), part(self.far, 2), part(self.far, 3), self.end,
        ]


class Ticks:
    def __init__(self):
        self.todo = []

    def add(self, key, fn):
        self.todo.append((key, len(self.todo), fn))
        self.todo.sort(key=lambda e: e[:2])

    def run(self, count=1):
        for _ in range(min(count, len(self.todo))):
            self.todo.pop(0)[2]()

    def until(self, fn):
        while any(e[2] == fn for e in self.todo):
            self.run()


ATT = dict(
    q=((2048, 64), BF), k=((2048, 64), BF), v=((2048, 64), BF), g=((2048, 64), BF),
    kt=((64, 2048), BF), vt=((80, 2048), BF), gt=((64, 2048), F32),
    dkv=((2048, 128), F32), mx=((8, TQ), F32), st=((4, TQ, TQ), F32), e=((4, TQ, TQ), BF),
    ot=((80, TQ), F32), dq=((64, TQ), F32), g2=((TQ, 64), BF),
)


def split_heads(recv, seq, b):
    @pl.loop(0, 8)
    def _(i):
        part = recv[i, pl.ds(seq * 256, 256), :]
        rows = pl.ds(i * 256, 256)
        q, k, v, g = (part[:, 64 * n : 64 * n + 64] for n in range(4))
        b.q[rows, :] = q
        b.k[rows, :] = k
        b.v[rows, :] = v
        b.g[rows, :] = g
        cols = pl.ds(pl.multiple_of(i * 256, 256), 256)
        b.kt[:, cols] = k.astype(F32).T.astype(BF)
        b.vt[0:64, cols] = v.astype(F32).T.astype(BF)
        b.gt[:, cols] = g.astype(F32).T

    b.vt[64:80, :] = jnp.ones((16, 2048), BF)
    b.dkv[...] = jnp.zeros(b.dkv.shape, F32)


def attend_block(qi, seq, b, send, tick):
    scale = 0.125 * LOG2E
    qrows = slice(qi * TQ, (qi + 1) * TQ)
    q = b.q[qrows, :]
    b.mx[...] = jnp.full((8, TQ), -1e30, F32)

    def scores(j, masked):
        st = dot_nt(b.k[pl.ds(j * TQ, TQ), :], q)
        if masked:
            key = lax.broadcasted_iota(jnp.int32, (TQ, TQ), 0)
            query = lax.broadcasted_iota(jnp.int32, (TQ, TQ), 1)
            st = jnp.where(key <= query, st, -1e30)
        b.st[j] = st
        b.mx[...] = jnp.maximum(b.mx[...], jnp.max(st.reshape(TQ // 8, 8, TQ), axis=0))

    if qi > 0:

        @pl.loop(0, qi)
        def _(j):
            scores(j, False)

    scores(qi, True)
    top = jnp.max(b.mx[...], axis=0, keepdims=True) * scale
    tick()
    b.ot[...] = jnp.zeros(b.ot.shape, F32)

    @pl.loop(0, qi + 1)
    def _(j):
        e = jnp.exp2(b.st[j] * scale - top).astype(BF)
        b.e[j] = e
        b.ot[...] += dot_nn(b.vt[:, pl.ds(pl.multiple_of(j * TQ, TQ), TQ)], e)

    inv = 1.0 / b.ot[64:65, :]
    out = b.ot[0:64, :] * inv
    gt = b.gt[:, qrows] * inv
    inner = jnp.sum(out * gt, axis=0, keepdims=True)
    b.g2[...] = gt.T.astype(BF)
    tick()
    b.dq[...] = jnp.zeros(b.dq.shape, F32)

    @pl.loop(0, qi + 1)
    def _(j):
        rows = pl.ds(j * TQ, TQ)
        g2 = b.g2[...]
        dp = dot_nt(b.v[rows, :], g2)
        e = b.e[j]
        ds = (e.astype(F32) * (dp - inner)).astype(BF)
        b.dkv[rows, 0:64] += dot_nn(ds, b.q[qrows, :])
        b.dkv[rows, 64:128] += dot_nn(e, g2)
        b.dq[...] += dot_nn(b.kt[:, pl.ds(pl.multiple_of(j * TQ, TQ), TQ)], ds)

    both = jnp.concatenate([out, b.dq[...] * 0.125], axis=0).T.astype(BF)
    for h in range(2):
        send[qi * 2 + h, seq * 256 : (seq + 1) * 256, 0:128] = both[h * 256 : (h + 1) * 256]
    tick()


def finish_heads(seq, b, send):
    @pl.loop(0, 8)
    def _(i):
        t = b.dkv[pl.ds(i * 256, 256), :]
        lane = lax.broadcasted_iota(jnp.int32, t.shape, 1)
        send[i, pl.ds(seq * 256, 256), 128:256] = (t * jnp.where(lane < 64, 0.125, 1.0)).astype(BF)


def turn(a, cos, low, high):
    return a * cos + pltpu.roll(a, 112, 1) * low + pltpu.roll(a, 16, 1) * high


K1 = dict(
    wa=((32, 64, 2048), BF), wb=((32, 64, 2048), BF), wc=((32, 64, 2048), BF),
    hid=((512, 2048), BF), gv=((512, 2048), BF), act=((512, 2048), BF), din=((512, 2048), BF),
    hs=((8, 512, 256), BF), hr=((8, 512, 256), BF), br=((8, 512, 256), BF), gp=((512, 2048), F32),
    dproj=((512, 1536), BF), att=((512, 512), BF), sums=((8, 2048), F32),
)


def block_kernel(
    x_hbm, g_hbm, sa, sb, sc, gain, shift, bqkv, bfc1, cos, low, high,
    o_hid, o_act, o_din, o_dproj, o_att, o_norm, o_mixed, o_sums, *refs,
):
    names = list(K1) + list(ATT)
    m = Scratch(names, refs[: len(names)])
    wsend, wrecv, wlocal, asend, arecv, local, lout = refs[len(names) :]
    p = Place()
    barrier([p.sp_peer(k) for k in range(1, 8)] + [p.dev(p.x, (p.y + k) % 4, p.c, p.z) for k in (1, 3)] + [p.sibling()])
    ga, gb, gc = (
        Gather(p, s, w, wsend.at[i], wrecv.at[i], wlocal.at[i]) for i, (s, w) in enumerate(((sa, m.wa), (sb, m.wb), (sc, m.wc)))
    )
    ga.start()
    gb.start()
    load_x = pltpu.make_async_copy(x_hbm, m.act, local.at[0])
    load_g = pltpu.make_async_copy(g_hbm, m.gv, local.at[1])
    load_x.start()
    load_g.start()
    ticks = Ticks()
    for i, g in enumerate((ga, gb)):
        for k, t in enumerate(g.ticks()):
            ticks.add(i * 9 + k, t)

    load_x.wait()

    def norm_rows(n):
        @pl.loop(0, 4)
        def _(r):
            rows = pl.ds(n * 128 + r * 32, 32)
            x = m.act[rows, :].astype(F32)
            cent = x - jnp.mean(x, axis=-1, keepdims=True)
            inv = lax.rsqrt(jnp.mean(cent * cent, axis=-1, keepdims=True) + 1e-05)
            m.hid[rows, :] = (cent * inv * gain[...] + shift[...]).astype(BF)

    for n in range(4):
        norm_rows(n)
        if n > 1:
            ticks.run()
    outs = []

    def put(src, dst):
        c = pltpu.make_async_copy(src, dst, lout.at[len(outs)])
        c.start()
        outs.append(c)

    put(m.hid, o_hid)
    load_g.wait()

    @pl.loop(0, 8)
    def _(n):
        cols = pl.ds(pl.multiple_of(n * 256, 256), 256)
        m.sums[2:3, cols] = jnp.sum(m.gv[:, cols].astype(F32), axis=0, keepdims=True)

    ticks.until(ga.end)

    for part in range(4):
        for t in range(2):
            col = part * 512 + t * 256
            lhs = m.gv if part == 3 else m.hid
            acc = dot_nn(lhs[...], m.wa[:, :, col : col + 256].reshape(2048, 256))
            if part < 3:
                acc = acc + bqkv[:, col : col + 256]
            for sq in range(2):
                for lh in range(2):
                    a = acc[sq * 256 : (sq + 1) * 256, lh * 128 : (lh + 1) * 128]
                    if part < 2:
                        a = turn(a, cos[...], low[...], high[...])
                    a = a.astype(BF)
                    for e in range(2):
                        m.hs[t * 4 + lh * 2 + e, sq * 256 : (sq + 1) * 256, part * 64 : part * 64 + 64] = a[:, e * 64 : e * 64 + 64]
            if t:
                ticks.run()

    def exchange(dst, recv, seq, base):
        rows = pl.ds(seq * 256, 256)
        for k in range(1, 8):
            to = (p.s + k) % 8
            remote(m.hs.at[to, rows], dst.at[p.s, rows], asend.at[base], recv, p.sp_peer(k))
        c = pltpu.make_async_copy(m.hs.at[p.s, rows], dst.at[p.s, rows], local.at[2 + base])
        c.start()
        return c

    def exchanged(dst, recv, seq, own):
        wait_bytes(dst.at[pl.ds(0, 7), pl.ds(seq * 256, 256)], recv)
        own.wait()

    def sent(base):
        wait_bytes(m.hs.at[pl.ds(0, 7), pl.ds(0, 256)], asend.at[base])

    own = [exchange(m.hr, arecv.at[seq], seq, seq) for seq in range(2)]
    gc.start()
    for k, t in enumerate(gc.ticks()):
        ticks.add(19 + k, t)
    ticks.until(gb.end)

    def hidden_units(n):
        cols = slice(n * 256, n * 256 + 256)
        u = dot_nn(m.hid[...], m.wb[:, :, cols].reshape(2048, 256)) + bfc1[:, cols]
        k = math.sqrt(2.0 / math.pi)
        sq = u * u
        th = jnp.tanh(u * (k + (k * 0.044715) * sq))
        half = 0.5 + 0.5 * th
        m.act[:, cols] = (u * half).astype(BF)
        m.gp[:, cols] = half + (0.5 * u) * (1.0 - th * th) * (k + (3.0 * k * 0.044715) * sq)

    for n in range(8):
        hidden_units(n)
        if n % 2:
            ticks.run()
    put(m.act, o_act)

    back = []
    for seq in range(2):
        exchanged(m.hr, arecv.at[seq], seq, own[seq])
        split_heads(m.hr, seq, m)
        if seq == 0:
            sent(0)
            sent(1)
        for qi in range(4):
            attend_block(qi, seq, m, m.hs, ticks.run)
        finish_heads(seq, m, m.hs)
        back.append(exchange(m.br, arecv.at[2 + seq], seq, 2 + seq))
    ticks.until(gc.end)

    for n in range(8):
        cols = slice(n * 256, n * 256 + 256)
        ga_ = dot_nn(m.gv[...], m.wc[:, :, cols].reshape(2048, 256))
        d = (ga_ * m.gp[:, cols]).astype(BF)
        m.din[:, cols] = d
        m.sums[0:1, cols] = jnp.sum(d.astype(F32), axis=0, keepdims=True)
    put(m.din, o_din)

    @pl.loop(0, 4)
    def _(t):
        rows = pl.ds(t * 8, 8)
        cols = pl.ds(pl.multiple_of(t * 512, 512), 512)
        m.gp[:, cols] = dot_nt(m.act[...], m.wc[rows].reshape(512, 2048))
        m.st[t] = dot_nt(m.din[...], m.wb[rows].reshape(512, 2048))

    for seq in range(2):
        exchanged(m.br, arecv.at[2 + seq], seq, back[seq])

    for hp in range(4):
        pair = [m.br[2 * hp + e] for e in range(2)]
        for n in range(4):
            a = jnp.concatenate([pair[e][:, n * 64 : n * 64 + 64] for e in range(2)], axis=1)
            cols = slice(hp * 128, hp * 128 + 128)
            if n == 0:
                m.att[:, cols] = a
                continue
            if n < 3:
                a = a.astype(F32)
                a = jnp.concatenate(
                    [turn(a[sq * 256 : sq * 256 + 256], cos[...], -low[...], -high[...]) for sq in range(2)], axis=0
                ).astype(BF)
            cols = slice((n - 1) * 512 + hp * 128, (n - 1) * 512 + hp * 128 + 128)
            m.dproj[:, cols] = a
            m.sums[1:2, cols] = jnp.sum(a.astype(F32), axis=0, keepdims=True)
    put(m.att, o_att)
    put(m.dproj, o_dproj)
    outs[0].wait()

    @pl.loop(0, 4)
    def _(t):
        rows = pl.ds(t * 8, 8)
        cols = pl.ds(pl.multiple_of(t * 512, 512), 512)
        norm = m.st[t] + dot_nt(m.dproj[...], m.wa[rows, :, 0:1536].reshape(512, 1536))
        m.hid[:, cols] = norm.astype(BF)
        mixed = m.gp[:, cols] + dot_nt(m.att[...], m.wa[rows, :, 1536:2048].reshape(512, 512))
        m.gv[:, cols] = mixed.astype(BF)

    put(m.hid, o_norm)
    put(m.gv, o_mixed)
    put(m.sums, o_sums)
    for g in (ga, gb, gc):
        g.drain()
    sent(2)
    sent(3)
    for c in outs[1:]:
        c.wait()


def run_block(x, g, sa, sb, sc, gain, shift, bqkv, bfc1, cos, low, high):
    hbm = pl.BlockSpec(memory_space=pl.ANY)
    vmem = pl.BlockSpec(memory_space=pltpu.VMEM)
    full = jax.ShapeDtypeStruct((512, 2048), BF)
    dma = pltpu.SemaphoreType.DMA
    return pl.pallas_call(
        block_kernel,
        out_shape=[
            full, full, full, jax.ShapeDtypeStruct((512, 1536), BF), jax.ShapeDtypeStruct((512, 512), BF), full, full,
            jax.ShapeDtypeStruct((8, 2048), F32),
        ],
        in_specs=[hbm] * 5 + [vmem] * 7,
        out_specs=[hbm] * 8,
        scratch_shapes=[pltpu.VMEM(*v) for v in (K1 | ATT).values()]
        + [dma((3,)), dma((3, 16)), dma((3,)), dma((4,)), dma((4,)), dma((6,)), dma((8,))],
        compiler_params=pltpu.CompilerParams(collective_id=0, has_side_effects=True, vmem_limit_bytes=60 * MIB),
        cost_estimate=pl.CostEstimate(flops=30 * 10**9, bytes_accessed=20 * 10**6, transcendentals=10**7),
    )(x, g, sa, sb, sc, gain, shift, bqkv, bfc1, cos, low, high)


def layer_norm(inputs, gain, shift):
    average = jnp.mean(inputs, axis=-1, keepdims=True)
    centered = inputs - average
    spread = jnp.mean(centered * centered, axis=-1, keepdims=True)
    return centered * lax.rsqrt(spread + 1e-05) * gain + shift


def contract_first(left, right):
    return lax.dot_general(left, right, (((0,), (0,)), ((), ())), preferred_element_type=F32)


def body(tokens, ln_gain, ln_bias, w_qkv, b_qkv, w_dense, b_dense, w_fc1, b_fc1, w_fc2, b_fc2, cotangent):
    seq_count, local_len, width = tokens.shape
    rows = seq_count * local_len
    x = tokens.reshape(rows, width)
    g = cotangent.reshape(rows, width)
    gain = ln_gain.astype(F32)
    shift = ln_bias.astype(F32)
    places = (lax.axis_index("sp") * local_len + jnp.arange(local_len, dtype=jnp.int32)).astype(F32)
    freqs = jnp.exp(jnp.arange(ROT // 2, dtype=F32) * (-2.0 * math.log(10000.0) / ROT))
    angle = places[:, None] * freqs[None, :]
    c, s = jnp.cos(angle), jnp.sin(angle)
    one, zero = jnp.ones((local_len, 32), F32), jnp.zeros((local_len, 16), F32)
    cos = jnp.concatenate([c, c, one] * 2, axis=1)
    low = jnp.concatenate([-s, zero, zero, zero] * 2, axis=1)
    high = jnp.concatenate([zero, s, zero, zero] * 2, axis=1)
    sa = jnp.concatenate([w_qkv.reshape(64, 1536), w_dense.T], axis=1)
    hid, act, din, dproj, att, norm, mixed, sums = run_block(
        x, g, sa, w_fc1, w_fc2.T, gain[None], shift[None], b_qkv.astype(F32).reshape(1, 1536), b_fc1.astype(F32)[None], cos, low, high
    )
    x32 = x.astype(F32)
    mixed_out = (
        (x32 + lax.psum(mixed, "tp").astype(F32) + b_dense.astype(F32) + b_fc2.astype(F32)).astype(BF).reshape(tokens.shape)
    )
    grad_normed = lax.psum(norm, "tp").astype(F32)
    grad_x, grad_gain, grad_shift = jax.vjp(layer_norm, x32, gain, shift)[1](grad_normed)
    grad_tokens = (g.astype(F32) + grad_x).astype(BF).reshape(tokens.shape)
    small = jnp.concatenate([grad_gain, grad_shift, sums[0], sums[2], sums[1, :1536]])
    small = lax.psum(small, ("fsdp", "sp"))
    scatter = functools.partial(lax.psum_scatter, axis_name=("fsdp", "sp"), tiled=True)
    gq = scatter(contract_first(hid, dproj).astype(BF), scatter_dimension=0).astype(F32).reshape(64, 3, 512)
    gd = scatter(contract_first(att, g).astype(BF), scatter_dimension=1).astype(F32)
    g1 = scatter(contract_first(hid, din).astype(BF), scatter_dimension=0).astype(F32)
    g2 = scatter(contract_first(act, g).astype(BF), scatter_dimension=1).astype(F32)
    out = small[6144:8192]
    return (
        mixed_out, grad_tokens, small[:2048], small[2048:4096], gq, small[8192:].reshape(3, 512), gd, out, g1,
        small[4096:6144], g2, out,
    )


def solution(mesh):
    both = ("fsdp", "sp")
    act = P("fsdp", "sp", None)
    in_specs = (
        act, P(), P(), P(both, None, "tp"), P(None, "tp"), P("tp", both), P(), P(both, "tp"), P("tp"), P("tp", both), P(), act,
    )
    out_specs = (
        act, act, P(), P(), P(both, None, "tp"), P(None, "tp"), P("tp", both), P(), P(both, "tp"), P("tp"), P("tp", both), P(),
    )
    return jax.shard_map(body, mesh=mesh, in_specs=in_specs, out_specs=out_specs, check_vma=False)
```

```python
import functools
import math

import jax
import jax.numpy as jnp
from jax import lax
from jax.experimental import pallas as pl
from jax.experimental.pallas import tpu as pltpu
from jax.sharding import PartitionSpec as P

MESH = pl.DeviceIdType.MESH
F32 = jnp.float32
BF = jnp.bfloat16
HDIM = 64
ROT = 32
TQ = 512
LOG2E = 1.4426950408889634
MIB = 2**20


def dot_nt(a, b):
    return lax.dot_general(a, b, (((1,), (1,)), ((), ())), preferred_element_type=F32)


def dot_nn(a, b):
    return lax.dot_general(a, b, (((1,), (0,)), ((), ())), preferred_element_type=F32)


class Scratch:
    def __init__(self, names, refs):
        for name, ref in zip(names, refs):
            setattr(self, name, ref)


class Place:
    def __init__(self):
        f, s, t = (lax.axis_index(a) for a in ("fsdp", "sp", "tp"))
        self.f, self.s = f, s
        self.x, self.y, self.c, self.z = s % 4, (s // 4) * 2 + f // 2, f % 2, t
        self.a1 = self.x * (1 - self.c) + self.y * self.c
        self.a2 = self.y * (1 - self.c) + self.x * self.c

    def xy(self, d1, d2):
        p1, p2, c = (self.a1 + d1 + 4) % 4, (self.a2 + d2 + 4) % 4, self.c
        return p1 * (1 - c) + p2 * c, p2 * (1 - c) + p1 * c

    def dev(self, x, y, c, z):
        return ((y % 2) * 2 + c, (y // 2) * 4 + x, z)

    def peer(self, d1, d2):
        x, y = self.xy(d1, d2)
        return self.dev(x, y, self.c, self.z)

    def sibling(self):
        return self.dev(self.x, self.y, 1 - self.c, self.z)

    def blk(self, d1, d2):
        x, y = self.xy(d1, d2)
        return ((y % 2) * 2 + self.c) * 8 + (y // 2) * 4 + x

    def zpeer(self, d):
        return self.dev(self.x, self.y, self.c, (self.z + d + 4) % 4)

    def sp_peer(self, k):
        return (self.f, (self.s + k) % 8, self.z)


def barrier(devices):
    sem = pltpu.get_barrier_semaphore()
    for d in devices:
        pl.semaphore_signal(sem, inc=1, device_id=d, device_id_type=MESH)
    pl.semaphore_wait(sem, len(devices))


def remote(src, dst, send, recv, device):
    pltpu.make_async_remote_copy(
        src_ref=src, dst_ref=dst, send_sem=send, recv_sem=recv, device_id=device, device_id_type=MESH
    ).start()


def wait_bytes(ref, sem):
    pltpu.make_async_copy(ref, ref, sem).wait()


STEP = (0, -1, 1, 2)


class Gather:
    def __init__(self, p, shard, w, send, recv, local):
        self.p, self.shard, self.w, self.send, self.recv, self.local = p, shard, w, send, recv, local

    def push(self, b, sem, device, half=None, src=None):
        dst = self.w.at[b] if half is None else self.w.at[b, pl.ds(32 * half, 32)]
        remote(dst if src is None else src, dst, self.send, self.recv.at[sem], device)

    def arrive(self, b, sem):
        wait_bytes(self.w.at[b], self.recv.at[sem])

    def start(self):
        p, s = self.p, self.shard
        own = p.blk(0, 0)
        for sem, device in ((0, p.peer(1, 0)), (1, p.peer(-1, 0)), (3, p.peer(0, 1)), (7, p.peer(0, -1)), (15, p.sibling())):
            self.push(own, sem, device, src=s)
        pltpu.make_async_copy(s, self.w.at[own], self.local).start()

    def second(self, j):
        p = self.p
        b = p.blk(STEP[j], 0)
        self.push(b, 3 + j, p.peer(0, 1))
        self.push(b, 7 + j, p.peer(0, -1))
        self.push(b, 15, p.sibling())

    def first_low(self):
        p = self.p
        b = p.blk(-1, 0)
        self.arrive(b, 0)
        self.push(b, 2, p.peer(1, 0), half=0)
        self.second(1)

    def first_high(self):
        p = self.p
        b = p.blk(1, 0)
        self.arrive(b, 1)
        self.push(b, 2, p.peer(-1, 0), half=1)
        self.second(2)

    def first_far(self):
        self.arrive(self.p.blk(2, 0), 2)
        self.second(3)

    def low(self, j):
        p = self.p
        b = p.blk(STEP[j], -1)
        self.arrive(b, 3 + j)
        self.push(b, 11 + j, p.peer(0, 1), half=0)
        self.push(b, 15, p.sibling())

    def high(self, j):
        p = self.p
        b = p.blk(STEP[j], 1)
        self.arrive(b, 7 + j)
        self.push(b, 11 + j, p.peer(0, -1), half=1)
        self.push(b, 15, p.sibling())

    def far(self, j):
        b = self.p.blk(STEP[j], 2)
        self.arrive(b, 11 + j)
        self.push(b, 15, self.p.sibling())

    def end(self):
        wait_bytes(self.w.at[pl.ds(0, 16)], self.recv.at[15])
        own = self.p.blk(0, 0)
        pltpu.make_async_copy(self.shard, self.w.at[own], self.local).wait()

    def drain(self):
        wait_bytes(self.w.at[pl.ds(0, 31)], self.send)

    def ticks(self):
        part = functools.partial
        return [
            self.first_low, self.first_high, part(self.low, 0), part(self.high, 0), self.first_far,
            part(self.low, 1), part(self.high, 1), part(self.far, 0), part(self.low, 2), part(self.high, 2), part(self.far, 1),
            part(self.low, 3), part(self.high, 3), part(self.far, 2), part(self.far, 3), self.end,
        ]


class Ticks:
    def __init__(self):
        self.todo = []

    def add(self, key, fn):
        self.todo.append((key, len(self.todo), fn))
        self.todo.sort(key=lambda e: e[:2])

    def run(self, count=1):
        for _ in range(min(count, len(self.todo))):
            self.todo.pop(0)[2]()

    def until(self, fn):
        while any(e[2] == fn for e in self.todo):
            self.run()


ATT = dict(
    q=((2048, 64), BF), k=((2048, 64), BF), v=((2048, 64), BF), g=((2048, 64), BF),
    kt=((64, 2048), BF), vt=((80, 2048), BF), gt=((64, 2048), F32),
    dkv=((2048, 128), F32), mx=((8, TQ), F32), st=((4, TQ, TQ), F32), e=((4, TQ, TQ), BF),
    ot=((80, TQ), F32), dq=((64, TQ), F32), g2=((TQ, 64), BF),
)


def split_heads(recv, seq, b):
    @pl.loop(0, 8)
    def _(i):
        part = recv[i, pl.ds(seq * 256, 256), :]
        rows = pl.ds(i * 256, 256)
        q, k, v, g = (part[:, 64 * n : 64 * n + 64] for n in range(4))
        b.q[rows, :] = q
        b.k[rows, :] = k
        b.v[rows, :] = v
        b.g[rows, :] = g
        cols = pl.ds(pl.multiple_of(i * 256, 256), 256)
        b.kt[:, cols] = k.astype(F32).T.astype(BF)
        b.vt[0:64, cols] = v.astype(F32).T.astype(BF)
        b.gt[:, cols] = g.astype(F32).T

    b.vt[64:80, :] = jnp.ones((16, 2048), BF)
    b.dkv[...] = jnp.zeros(b.dkv.shape, F32)


def attend_block(qi, seq, b, send, tick):
    scale = 0.125 * LOG2E
    qrows = slice(qi * TQ, (qi + 1) * TQ)
    q = b.q[qrows, :]
    b.mx[...] = jnp.full((8, TQ), -1e30, F32)

    def scores(j, masked):
        st = dot_nt(b.k[pl.ds(j * TQ, TQ), :], q)
        if masked:
            key = lax.broadcasted_iota(jnp.int32, (TQ, TQ), 0)
            query = lax.broadcasted_iota(jnp.int32, (TQ, TQ), 1)
            st = jnp.where(key <= query, st, -1e30)
        b.st[j] = st
        b.mx[...] = jnp.maximum(b.mx[...], jnp.max(st.reshape(TQ // 8, 8, TQ), axis=0))

    if qi > 0:

        @pl.loop(0, qi)
        def _(j):
            scores(j, False)

    scores(qi, True)
    top = jnp.max(b.mx[...], axis=0, keepdims=True) * scale
    tick()
    b.ot[...] = jnp.zeros(b.ot.shape, F32)

    @pl.loop(0, qi + 1)
    def _(j):
        e = jnp.exp2(b.st[j] * scale - top).astype(BF)
        b.e[j] = e
        b.ot[...] += dot_nn(b.vt[:, pl.ds(pl.multiple_of(j * TQ, TQ), TQ)], e)

    inv = 1.0 / b.ot[64:65, :]
    out = b.ot[0:64, :] * inv
    gt = b.gt[:, qrows] * inv
    inner = jnp.sum(out * gt, axis=0, keepdims=True)
    b.g2[...] = gt.T.astype(BF)
    tick()
    b.dq[...] = jnp.zeros(b.dq.shape, F32)

    @pl.loop(0, qi + 1)
    def _(j):
        rows = pl.ds(j * TQ, TQ)
        g2 = b.g2[...]
        dp = dot_nt(b.v[rows, :], g2)
        e = b.e[j]
        ds = (e.astype(F32) * (dp - inner)).astype(BF)
        b.dkv[rows, 0:64] += dot_nn(ds, b.q[qrows, :])
        b.dkv[rows, 64:128] += dot_nn(e, g2)
        b.dq[...] += dot_nn(b.kt[:, pl.ds(pl.multiple_of(j * TQ, TQ), TQ)], ds)

    both = jnp.concatenate([out, b.dq[...] * 0.125], axis=0).T.astype(BF)
    for h in range(2):
        send[qi * 2 + h, seq * 256 : (seq + 1) * 256, 0:128] = both[h * 256 : (h + 1) * 256]
    tick()


def finish_heads(seq, b, send):
    @pl.loop(0, 8)
    def _(i):
        t = b.dkv[pl.ds(i * 256, 256), :]
        lane = lax.broadcasted_iota(jnp.int32, t.shape, 1)
        send[i, pl.ds(seq * 256, 256), 128:256] = (t * jnp.where(lane < 64, 0.125, 1.0)).astype(BF)


def turn(a, cos, low, high):
    return a * cos + pltpu.roll(a, 112, 1) * low + pltpu.roll(a, 16, 1) * high


K1 = dict(
    wa=((32, 64, 2048), BF), wb=((32, 64, 2048), BF), wc=((32, 64, 2048), BF),
    hid=((512, 2048), BF), gv=((512, 2048), BF), act=((512, 2048), BF), din=((512, 2048), BF),
    hs=((8, 512, 256), BF), hr=((8, 512, 256), BF), br=((8, 512, 256), BF), gp=((512, 2048), F32),
    dproj=((512, 1536), BF), att=((512, 512), BF), sums=((8, 2048), F32),
)


def block_kernel(
    x_hbm, g_hbm, sa, sb, sc, gain, shift, bqkv, bfc1, cos, low, high,
    o_ht, o_gt, o_act, o_din, o_dproj, o_att, o_norm, o_mixed, o_sums, *refs,
):
    names = list(K1) + list(ATT)
    m = Scratch(names, refs[: len(names)])
    wsend, wrecv, wlocal, asend, arecv, local, lout = refs[len(names) :]
    p = Place()
    barrier([p.sp_peer(k) for k in range(1, 8)] + [p.dev(p.x, (p.y + k) % 4, p.c, p.z) for k in (1, 3)] + [p.sibling()])
    ga, gb, gc = (
        Gather(p, s, w, wsend.at[i], wrecv.at[i], wlocal.at[i]) for i, (s, w) in enumerate(((sa, m.wa), (sb, m.wb), (sc, m.wc)))
    )
    ga.start()
    gb.start()
    load_x = pltpu.make_async_copy(x_hbm, m.act, local.at[0])
    load_g = pltpu.make_async_copy(g_hbm, m.gv, local.at[1])
    load_x.start()
    load_g.start()
    ticks = Ticks()
    for i, g in enumerate((ga, gb)):
        for k, t in enumerate(g.ticks()):
            ticks.add(i * 9 + k, t)

    load_x.wait()

    def norm_rows(n):
        @pl.loop(0, 4)
        def _(r):
            rows = pl.ds(n * 128 + r * 32, 32)
            x = m.act[rows, :].astype(F32)
            cent = x - jnp.mean(x, axis=-1, keepdims=True)
            inv = lax.rsqrt(jnp.mean(cent * cent, axis=-1, keepdims=True) + 1e-05)
            m.hid[rows, :] = (cent * inv * gain[...] + shift[...]).astype(BF)

    for n in range(4):
        norm_rows(n)
        if n > 1:
            ticks.run()
    outs = []

    def put(src, dst):
        c = pltpu.make_async_copy(src, dst, lout.at[len(outs)])
        c.start()
        outs.append(c)

    load_g.wait()

    def flip(src, dst, n):
        at, half = n // 2, n % 2
        dst[at * 2 + half] = src[half * 256 : half * 256 + 256, at * 512 : at * 512 + 512].astype(F32).T.astype(BF)

    for n in range(8):
        flip(m.gv, m.hs, n)
        if n % 4 == 3:
            ticks.run()
    put(m.hs, o_gt)
    for n in range(8):
        flip(m.hid, m.br, n)
        if n % 4 == 3:
            ticks.run()
    put(m.br, o_ht)

    @pl.loop(0, 8)
    def _(n):
        cols = pl.ds(pl.multiple_of(n * 256, 256), 256)
        m.sums[2:3, cols] = jnp.sum(m.gv[:, cols].astype(F32), axis=0, keepdims=True)

    ticks.until(ga.end)

    outs[0].wait()
    outs[1].wait()

    for part in range(4):
        for t in range(2):
            col = part * 512 + t * 256
            lhs = m.gv if part == 3 else m.hid
            acc = dot_nn(lhs[...], m.wa[:, :, col : col + 256].reshape(2048, 256))
            if part < 3:
                acc = acc + bqkv[:, col : col + 256]
            for sq in range(2):
                for lh in range(2):
                    a = acc[sq * 256 : (sq + 1) * 256, lh * 128 : (lh + 1) * 128]
                    if part < 2:
                        a = turn(a, cos[...], low[...], high[...])
                    a = a.astype(BF)
                    for e in range(2):
                        m.hs[t * 4 + lh * 2 + e, sq * 256 : (sq + 1) * 256, part * 64 : part * 64 + 64] = a[:, e * 64 : e * 64 + 64]
            if t:
                ticks.run()

    def exchange(dst, recv, seq, base):
        rows = pl.ds(seq * 256, 256)
        for k in range(1, 8):
            to = (p.s + k) % 8
            remote(m.hs.at[to, rows], dst.at[p.s, rows], asend.at[base], recv, p.sp_peer(k))
        c = pltpu.make_async_copy(m.hs.at[p.s, rows], dst.at[p.s, rows], local.at[2 + base])
        c.start()
        return c

    def exchanged(dst, recv, seq, own):
        wait_bytes(dst.at[pl.ds(0, 7), pl.ds(seq * 256, 256)], recv)
        own.wait()

    def sent(base):
        wait_bytes(m.hs.at[pl.ds(0, 7), pl.ds(0, 256)], asend.at[base])

    own = [exchange(m.hr, arecv.at[seq], seq, seq) for seq in range(2)]
    gc.start()
    for k, t in enumerate(gc.ticks()):
        ticks.add(19 + k, t)
    ticks.until(gb.end)

    def hidden_units(n):
        cols = slice(n * 256, n * 256 + 256)
        u = dot_nn(m.hid[...], m.wb[:, :, cols].reshape(2048, 256)) + bfc1[:, cols]
        k = math.sqrt(2.0 / math.pi)
        sq = u * u
        th = jnp.tanh(u * (k + (k * 0.044715) * sq))
        half = 0.5 + 0.5 * th
        m.act[:, cols] = (u * half).astype(BF)
        m.gp[:, cols] = half + (0.5 * u) * (1.0 - th * th) * (k + (3.0 * k * 0.044715) * sq)

    for n in range(8):
        hidden_units(n)
        if n % 2:
            ticks.run()
    put(m.act, o_act)

    back = []
    for seq in range(2):
        exchanged(m.hr, arecv.at[seq], seq, own[seq])
        split_heads(m.hr, seq, m)
        if seq == 0:
            sent(0)
            sent(1)
        for qi in range(4):
            attend_block(qi, seq, m, m.hs, ticks.run)
        finish_heads(seq, m, m.hs)
        back.append(exchange(m.br, arecv.at[2 + seq], seq, 2 + seq))
    ticks.until(gc.end)

    for n in range(8):
        cols = slice(n * 256, n * 256 + 256)
        ga_ = dot_nn(m.gv[...], m.wc[:, :, cols].reshape(2048, 256))
        d = (ga_ * m.gp[:, cols]).astype(BF)
        m.din[:, cols] = d
        m.sums[0:1, cols] = jnp.sum(d.astype(F32), axis=0, keepdims=True)
    put(m.din, o_din)

    @pl.loop(0, 4)
    def _(t):
        rows = pl.ds(t * 8, 8)
        cols = pl.ds(pl.multiple_of(t * 512, 512), 512)
        m.gp[:, cols] = dot_nt(m.act[...], m.wc[rows].reshape(512, 2048))
        m.st[t] = dot_nt(m.din[...], m.wb[rows].reshape(512, 2048))

    for seq in range(2):
        exchanged(m.br, arecv.at[2 + seq], seq, back[seq])

    for hp in range(4):
        pair = [m.br[2 * hp + e] for e in range(2)]
        for n in range(4):
            a = jnp.concatenate([pair[e][:, n * 64 : n * 64 + 64] for e in range(2)], axis=1)
            cols = slice(hp * 128, hp * 128 + 128)
            if n == 0:
                m.att[:, cols] = a
                continue
            if n < 3:
                a = a.astype(F32)
                a = jnp.concatenate(
                    [turn(a[sq * 256 : sq * 256 + 256], cos[...], -low[...], -high[...]) for sq in range(2)], axis=0
                ).astype(BF)
            cols = slice((n - 1) * 512 + hp * 128, (n - 1) * 512 + hp * 128 + 128)
            m.dproj[:, cols] = a
            m.sums[1:2, cols] = jnp.sum(a.astype(F32), axis=0, keepdims=True)
    put(m.att, o_att)
    put(m.dproj, o_dproj)

    @pl.loop(0, 4)
    def _(t):
        rows = pl.ds(t * 8, 8)
        cols = pl.ds(pl.multiple_of(t * 512, 512), 512)
        norm = m.st[t] + dot_nt(m.dproj[...], m.wa[rows, :, 0:1536].reshape(512, 1536))
        m.hid[:, cols] = norm.astype(BF)
        mixed = m.gp[:, cols] + dot_nt(m.att[...], m.wa[rows, :, 1536:2048].reshape(512, 512))
        m.gv[:, cols] = mixed.astype(BF)

    put(m.hid, o_norm)
    put(m.gv, o_mixed)
    put(m.sums, o_sums)
    for g in (ga, gb, gc):
        g.drain()
    sent(2)
    sent(3)
    for c in outs[2:]:
        c.wait()


def run_block(x, g, sa, sb, sc, gain, shift, bqkv, bfc1, cos, low, high):
    hbm = pl.BlockSpec(memory_space=pl.ANY)
    vmem = pl.BlockSpec(memory_space=pltpu.VMEM)
    full = jax.ShapeDtypeStruct((512, 2048), BF)
    flipped = jax.ShapeDtypeStruct((8, 512, 256), BF)
    dma = pltpu.SemaphoreType.DMA
    return pl.pallas_call(
        block_kernel,
        out_shape=[
            flipped, flipped, full, full, jax.ShapeDtypeStruct((512, 1536), BF), jax.ShapeDtypeStruct((512, 512), BF), full, full,
            jax.ShapeDtypeStruct((8, 2048), F32),
        ],
        in_specs=[hbm] * 5 + [vmem] * 7,
        out_specs=[hbm] * 9,
        scratch_shapes=[pltpu.VMEM(*v) for v in (K1 | ATT).values()]
        + [dma((3,)), dma((3, 16)), dma((3,)), dma((4,)), dma((4,)), dma((6,)), dma((9,))],
        compiler_params=pltpu.CompilerParams(collective_id=0, has_side_effects=True, vmem_limit_bytes=60 * MIB),
        cost_estimate=pl.CostEstimate(flops=30 * 10**9, bytes_accessed=20 * 10**6, transcendentals=10**7),
    )(x, g, sa, sb, sc, gain, shift, bqkv, bfc1, cos, low, high)


FAR_FIRST = (2, 1, -1, 0)


class Scatter:
    def __init__(self, p, product, sbuf, r, half, full, half1, full1, ssend, srecv, send, recv):
        self.p, self.product = p, product
        self.sbuf, self.r, self.half, self.full, self.half1, self.full1 = sbuf, r, half, full, half1, full1
        self.ssend, self.srecv, self.send, self.recv = ssend, srecv, send, recv

    def group(self, d):
        y = (self.p.y + d + 4) % 4
        return (y % 2) * 2 + y // 2

    def rb(self, d1, d2):
        x, y = self.p.xy(d1, d2)
        return ((y % 2) * 2 + y // 2) * 4 + x

    def hand_over(self, n):
        k = self.group(FAR_FIRST[n])
        blocks = pl.ds(k * 4, 4)

        def store(cols, value):
            self.sbuf[blocks, :, cols] = value.astype(BF).reshape(4, 64, value.shape[1])

        self.product(k, 1 - self.p.c, store)
        remote(self.sbuf.at[blocks], self.r.at[blocks], self.ssend, self.srecv.at[n], self.p.sibling())

    def handed_over(self):
        wait_bytes(self.sbuf, self.ssend)

    def own_group(self, n):
        k = self.group(FAR_FIRST[n])
        blocks = pl.ds(k * 4, 4)
        wait_bytes(self.r.at[blocks], self.srecv.at[n])

        def store(cols, value):
            total = value.reshape(4, 64, value.shape[1]) + self.r[blocks, :, cols].astype(F32)
            self.r[blocks, :, cols] = total.astype(BF)

        self.product(k, self.p.c, store)

    def add(self, dst, src):
        dst[...] = (dst[...].astype(F32) + src[...].astype(F32)).astype(BF)

    def rows(self, d1, d2, h):
        return self.r.at[self.rb(d1, d2), pl.ds(32 * h, 32)]

    def far(self, j):
        p, d = self.p, FAR_FIRST[j]
        for h, to in ((0, 1), (1, -1)):
            remote(self.rows(d, 2, h), self.half.at[j, h], self.send, self.recv.at[2 * j + h], p.peer(0, to))

    def near(self, j):
        p, d = self.p, FAR_FIRST[j]
        for h, to in ((0, 1), (1, -1)):
            wait_bytes(self.half.at[j, h], self.recv.at[2 * j + h])
            self.add(self.rows(d, to, h), self.half.at[j, h])
            remote(self.r.at[self.rb(d, to)], self.full.at[j, h], self.send, self.recv.at[8 + 2 * j + h], p.peer(0, to))

    def sum(self, j):
        for h in range(2):
            wait_bytes(self.full.at[j, h], self.recv.at[8 + 2 * j + h])
        dst = self.r.at[self.rb(FAR_FIRST[j], 0)]
        dst[...] = (dst[...].astype(F32) + self.full[j, 0].astype(F32) + self.full[j, 1].astype(F32)).astype(BF)

    def far1(self):
        for h, to in ((0, 1), (1, -1)):
            remote(self.rows(2, 0, h), self.half1.at[h], self.send, self.recv.at[16 + h], self.p.peer(to, 0))

    def near1(self):
        for h, to in ((0, 1), (1, -1)):
            wait_bytes(self.half1.at[h], self.recv.at[16 + h])
            self.add(self.rows(to, 0, h), self.half1.at[h])
            remote(self.r.at[self.rb(to, 0)], self.full1.at[h], self.send, self.recv.at[18 + h], self.p.peer(to, 0))

    def sum1(self, out):
        for h in range(2):
            wait_bytes(self.full1.at[h], self.recv.at[18 + h])
        out[...] = self.r[self.rb(0, 0)].astype(F32) + self.full1[0].astype(F32) + self.full1[1].astype(F32)

    def drain(self):
        wait_bytes(self.r.at[pl.ds(0, 15)], self.send)


class Depth:
    def __init__(self, p, a, half, full, out, rsend, gsend, recv):
        self.p, self.a, self.half, self.full, self.out = p, a, half, full, out
        self.rsend, self.gsend, self.recv = rsend, gsend, recv

    def rows(self, ref, d, h=None):
        z = (self.p.z + d + 4) % 4
        return ref.at[pl.ds(z * 128, 128)] if h is None else ref.at[pl.ds(z * 128 + 64 * h, 64)]

    def far(self):
        for h, to in ((0, 1), (1, -1)):
            remote(self.rows(self.a, 2, h), self.half.at[h], self.rsend, self.recv.at[h], self.p.zpeer(to))

    def near(self):
        for h, to in ((0, 1), (1, -1)):
            wait_bytes(self.half.at[h], self.recv.at[h])
            dst = self.rows(self.a, to, h)
            dst[...] = (dst[...].astype(F32) + self.half[h].astype(F32)).astype(BF)
            remote(self.rows(self.a, to), self.full.at[h], self.rsend, self.recv.at[2 + h], self.p.zpeer(to))

    def arrived(self):
        for h in range(2):
            wait_bytes(self.full.at[h], self.recv.at[2 + h])

    def total(self, r):
        own = self.a[pl.ds(self.p.z * 128 + r, 32), :].astype(F32)
        return own + self.full[0, pl.ds(r, 32), :].astype(F32) + self.full[1, pl.ds(r, 32), :].astype(F32)

    def give(self):
        src = self.rows(self.out, 0)
        for h, to in ((0, 1), (1, -1)):
            remote(src, src, self.gsend, self.recv.at[4 + h], self.p.zpeer(to))

    def give_on(self):
        for h, to in ((0, 1), (1, -1)):
            wait_bytes(self.rows(self.out, -to), self.recv.at[4 + h])
            src = self.rows(self.out, -to, h)
            remote(src, src, self.gsend, self.recv.at[6], self.p.zpeer(to))

    def given(self):
        wait_bytes(self.rows(self.out, 2), self.recv.at[6])

    def drain(self):
        for sem in (self.rsend, self.gsend):
            wait_bytes(self.a.at[pl.ds(0, 384)], sem)


FULL = ((512, 2048), BF)
K2 = dict(
    ht=((8, 512, 256), BF), gt=((8, 512, 256), BF), act=FULL, din=FULL, dproj=((512, 1536), BF), att=((512, 512), BF),
    norm=FULL, mixed=FULL, xr=((128, 2048), BF), gr=((128, 2048), BF), oz=((2, 512, 2048), BF),
    zh=((2, 2, 64, 2048), BF), zf=((2, 2, 128, 2048), BF),
    sbuf=((2, 16, 64, 2048), BF), r=((3, 16, 64, 2048), BF),
    half=((3, 4, 2, 32, 2048), BF), full=((3, 4, 2, 64, 2048), BF), half1=((3, 2, 32, 2048), BF), full1=((3, 2, 64, 2048), BF),
    res=((3, 64, 2048), F32), vec=((5, 8, 2048), F32), vin=((10, 8, 2048), F32),
)


def grad_kernel(
    ht, gt, act, din, dproj, att, norm, mixed, x, g, sums, gain, bout,
    o_mixed, o_tok, o_a, o_b, o_c, o_vec, *refs,
):
    m = Scratch(K2, refs[: len(K2)])
    load, lout, ssend, srecv, send, recv, zrs, zgs, zrecv, vsend, vrecv = refs[len(K2) :]
    p = Place()
    zrow = pl.ds(p.z * 128, 128)
    loads = {}
    for n, (src, dst) in dict(
        norm=(norm, m.norm), gt=(gt, m.gt), act=(act, m.act), ht=(ht, m.ht), din=(din, m.din), mixed=(mixed, m.mixed),
        xr=(x.at[zrow], m.xr), gr=(g.at[zrow], m.gr), dproj=(dproj, m.dproj), att=(att, m.att),
    ).items():
        loads[n] = pltpu.make_async_copy(src, dst, load.at[len(loads)])
        loads[n].start()
    xs = [p.dev((p.x + k) % 4, p.y, p.c, p.z) for k in (1, 2, 3)]
    ys = [p.dev(p.x, (p.y + k) % 4, p.c, p.z) for k in (1, 2, 3)]
    zs = [p.zpeer(k) for k in (1, 2, 3)]
    barrier(xs + ys + zs + [p.sibling()])

    def product(pairs):
        def run(k, cc, store):
            def tile(left, right, col, dst):
                rows = pl.ds((k % 2) * 256, 256)
                at = ((k // 2) * 2 + cc) * 2
                lhs0, lhs1 = left[at, rows, :], left[at + 1, rows, :]
                store(dst, dot_nn(lhs0, right[0:256, col]) + dot_nn(lhs1, right[256:512, col]))

            for left, right, start, count in pairs:
                @pl.loop(0, count)
                def _(t):
                    tile(left, right, pl.ds(pl.multiple_of(t * 512, 512), 512), pl.ds(pl.multiple_of(start + t * 512, 512), 512))

        return run

    pairs = ([(m.gt, m.act, 0, 4)], [(m.ht, m.din, 0, 4)], [(m.ht, m.dproj, 0, 3), (m.gt, m.att, 1536, 1)])
    sc = [
        Scatter(
            p, product(pr), m.sbuf.at[i % 2], m.r.at[i], m.half.at[i], m.full.at[i], m.half1.at[i], m.full1.at[i],
            ssend.at[i], srecv.at[i], send.at[i], recv.at[i],
        )
        for i, pr in enumerate(pairs)
    ]
    zn, zm = (
        Depth(p, a, m.zh.at[i], m.zf.at[i], m.oz.at[i], zrs.at[i], zgs.at[i], zrecv.at[i]) for i, a in enumerate((m.norm, m.mixed))
    )
    puts = []

    def put(src, dst):
        c = pltpu.make_async_copy(src, dst, lout.at[len(puts)])
        c.start()
        puts.append(c)

    loads["norm"].wait()
    zn.far()
    loads["gt"].wait()
    loads["act"].wait()
    for n in range(4):
        sc[0].hand_over(n)
    zn.near()
    loads["mixed"].wait()
    zm.far()
    for n in range(4):
        sc[0].own_group(n)
        if n == 0:
            loads["ht"].wait()
            loads["din"].wait()
    for j in range(4):
        sc[0].far(j)
    for n in range(4):
        sc[1].hand_over(n)
    sc[0].near(0)
    sc[0].near(1)
    zm.near()
    zn.arrived()
    for n in ("xr", "gr"):
        loads[n].wait()
    v = m.vec.at[0]
    v[...] = jnp.zeros((8, 2048), F32)

    def norm_back(i):
        r = i * 32
        x32 = m.xr[pl.ds(r, 32), :].astype(F32)
        cent = x32 - jnp.mean(x32, axis=-1, keepdims=True)
        inv = lax.rsqrt(jnp.mean(cent * cent, axis=-1, keepdims=True) + 1e-05)
        xn = cent * inv
        gn = zn.total(r)
        v[0:1, :] += jnp.sum(gn * xn, axis=0, keepdims=True)
        v[1:2, :] += jnp.sum(gn, axis=0, keepdims=True)
        gn = gn * gain[...]
        gx = inv * (gn - jnp.mean(gn, axis=-1, keepdims=True) - xn * jnp.mean(gn * xn, axis=-1, keepdims=True))
        m.oz[0, pl.ds(p.z * 128 + r, 32), :] = (m.gr[pl.ds(r, 32), :].astype(F32) + gx).astype(BF)

    @pl.loop(0, 4)
    def _(i):
        norm_back(i)

    zn.give()
    v[2:3, :] = sums[2:3, :]
    v[3:4, :] = sums[0:1, :]
    v[4:5, :] = sums[1:2, :]

    def vsends(stage, peers, base):
        for i, d in enumerate(peers):
            remote(m.vec.at[stage], m.vin.at[base + i], vsend, vrecv.at[base + i], d)

    def vsum(stage, count, base, rows):
        total = m.vec[stage]
        for i in range(count):
            wait_bytes(m.vin.at[base + i], vrecv.at[base + i])
            part = m.vin[base + i]
            if rows < 8:
                part = jnp.where(lax.broadcasted_iota(jnp.int32, part.shape, 0) < rows, part, 0.0)
            total = total + part
        m.vec[stage + 1] = total

    vsends(0, zs, 0)
    sc[0].near(2)
    sc[0].near(3)
    for n in range(4):
        sc[1].own_group(n)
    for j in range(4):
        sc[1].far(j)
    sc[0].sum(0)
    sc[0].far1()
    zm.arrived()

    @pl.loop(0, 4)
    def _(i):
        r = i * 32
        total = zm.total(r) + m.xr[pl.ds(r, 32), :].astype(F32) + bout[...]
        m.oz[1, pl.ds(p.z * 128 + r, 32), :] = total.astype(BF)

    zm.give()
    loads["dproj"].wait()
    loads["att"].wait()
    sc[0].handed_over()
    for n in range(4):
        sc[2].hand_over(n)
    vsum(0, 3, 0, 2)
    vsends(1, ys, 3)
    for j in range(4):
        sc[1].near(j)
    sc[0].sum(1)
    sc[0].sum(2)
    sc[0].near1()
    sc[0].sum(3)
    zn.give_on()
    for n in range(4):
        sc[2].own_group(n)
    for j in range(4):
        sc[2].far(j)
    vsum(1, 3, 3, 8)
    vsends(2, xs, 6)
    sc[0].sum1(m.res.at[0])
    put(m.res.at[0], o_c)
    sc[1].sum(0)
    sc[1].far1()
    for j in range(4):
        sc[2].near(j)
    zm.give_on()
    sc[1].sum(1)
    sc[1].sum(2)
    sc[1].near1()
    sc[1].sum(3)
    vsum(2, 3, 6, 8)
    vsends(3, [p.sibling()], 9)
    sc[2].sum(0)
    sc[2].far1()
    zn.given()
    put(m.oz.at[0], o_tok)
    sc[1].sum1(m.res.at[1])
    put(m.res.at[1], o_b)
    sc[2].sum(1)
    sc[2].sum(2)
    sc[2].near1()
    sc[2].sum(3)
    vsum(3, 1, 9, 8)
    put(m.vec.at[4], o_vec)
    zm.given()
    put(m.oz.at[1], o_mixed)
    sc[2].sum1(m.res.at[2])
    put(m.res.at[2], o_a)
    for s in sc:
        s.drain()
    for s in sc[1:]:
        s.handed_over()
    zn.drain()
    zm.drain()
    wait_bytes(m.vin, vsend)
    for c in puts:
        c.wait()


def run_grads(ht, gt, act, din, dproj, att, norm, mixed, x, g, sums, gain, bout):
    hbm = pl.BlockSpec(memory_space=pl.ANY)
    vmem = pl.BlockSpec(memory_space=pltpu.VMEM)
    full = jax.ShapeDtypeStruct((512, 2048), BF)
    shard = jax.ShapeDtypeStruct((64, 2048), F32)
    dma = pltpu.SemaphoreType.DMA
    return pl.pallas_call(
        grad_kernel,
        out_shape=[full, full, shard, shard, shard, jax.ShapeDtypeStruct((8, 2048), F32)],
        in_specs=[hbm] * 10 + [vmem] * 3,
        out_specs=[hbm] * 6,
        scratch_shapes=[pltpu.VMEM(*v) for v in K2.values()]
        + [dma((10,)), dma((6,)), dma((3,)), dma((3, 4)), dma((3,)), dma((3, 20)), dma((2,)), dma((2,)), dma((2, 7)), dma(()), dma((10,))],
        compiler_params=pltpu.CompilerParams(collective_id=1, has_side_effects=True, vmem_limit_bytes=60 * MIB),
        cost_estimate=pl.CostEstimate(flops=13 * 10**9, bytes_accessed=20 * 10**6, transcendentals=10**5),
    )(ht, gt, act, din, dproj, att, norm, mixed, x, g, sums, gain, bout)


def body(tokens, ln_gain, ln_bias, w_qkv, b_qkv, w_dense, b_dense, w_fc1, b_fc1, w_fc2, b_fc2, cotangent):
    seq_count, local_len, width = tokens.shape
    rows = seq_count * local_len
    x = tokens.reshape(rows, width)
    g = cotangent.reshape(rows, width)
    gain = ln_gain.astype(F32)
    shift = ln_bias.astype(F32)
    places = (lax.axis_index("sp") * local_len + jnp.arange(local_len, dtype=jnp.int32)).astype(F32)
    freqs = jnp.exp(jnp.arange(ROT // 2, dtype=F32) * (-2.0 * math.log(10000.0) / ROT))
    angle = places[:, None] * freqs[None, :]
    c, s = jnp.cos(angle), jnp.sin(angle)
    one, zero = jnp.ones((local_len, 32), F32), jnp.zeros((local_len, 16), F32)
    cos = jnp.concatenate([c, c, one] * 2, axis=1)
    low = jnp.concatenate([-s, zero, zero, zero] * 2, axis=1)
    high = jnp.concatenate([zero, s, zero, zero] * 2, axis=1)
    sa = jnp.concatenate([w_qkv.reshape(64, 1536), w_dense.T], axis=1)
    ht, gt, act, din, dproj, att, norm, mixed, sums = run_block(
        x, g, sa, w_fc1, w_fc2.T, gain[None], shift[None], b_qkv.astype(F32).reshape(1, 1536), b_fc1.astype(F32)[None], cos, low, high
    )
    bout = (b_dense.astype(F32) + b_fc2.astype(F32))[None]
    mixed_out, grad_tokens, ga, gb, gc, vec = run_grads(
        ht, gt, act, din, dproj, att, norm, mixed, x, g, sums, gain[None], bout
    )
    return (
        mixed_out.reshape(tokens.shape), grad_tokens.reshape(tokens.shape), vec[0], vec[1],
        ga[:, :1536].reshape(64, 3, 512), vec[4, :1536].reshape(3, 512), ga[:, 1536:].T, vec[2], gb, vec[3], gc.T, vec[2],
    )


def solution(mesh):
    both = ("fsdp", "sp")
    act = P("fsdp", "sp", None)
    in_specs = (
        act, P(), P(), P(both, None, "tp"), P(None, "tp"), P("tp", both), P(), P(both, "tp"), P("tp"), P("tp", both), P(), act,
    )
    out_specs = (
        act, act, P(), P(), P(both, None, "tp"), P(None, "tp"), P("tp", both), P(), P(both, "tp"), P("tp"), P("tp", both), P(),
    )
    return jax.shard_map(body, mesh=mesh, in_specs=in_specs, out_specs=out_specs, check_vma=False)
```

```python
import functools
import math

import jax
import jax.numpy as jnp
from jax import lax
from jax.experimental import pallas as pl
from jax.experimental.pallas import tpu as pltpu
from jax.sharding import PartitionSpec as P

MESH = pl.DeviceIdType.MESH
F32 = jnp.float32
BF = jnp.bfloat16
HDIM = 64
ROT = 32
TQ = 512
LOG2E = 1.4426950408889634
MIB = 2**20


def dot_nt(a, b):
    return lax.dot_general(a, b, (((1,), (1,)), ((), ())), preferred_element_type=F32)


def dot_nn(a, b):
    return lax.dot_general(a, b, (((1,), (0,)), ((), ())), preferred_element_type=F32)


class Scratch:
    def __init__(self, names, refs):
        for name, ref in zip(names, refs):
            setattr(self, name, ref)


class Place:
    def __init__(self):
        f, s, t = (lax.axis_index(a) for a in ("fsdp", "sp", "tp"))
        self.f, self.s = f, s
        self.x, self.y, self.c, self.z = s % 4, (s // 4) * 2 + f // 2, f % 2, t
        self.a1 = self.x * (1 - self.c) + self.y * self.c
        self.a2 = self.y * (1 - self.c) + self.x * self.c

    def xy(self, d1, d2):
        p1, p2, c = (self.a1 + d1 + 4) % 4, (self.a2 + d2 + 4) % 4, self.c
        return p1 * (1 - c) + p2 * c, p2 * (1 - c) + p1 * c

    def dev(self, x, y, c, z):
        return ((y % 2) * 2 + c, (y // 2) * 4 + x, z)

    def peer(self, d1, d2):
        x, y = self.xy(d1, d2)
        return self.dev(x, y, self.c, self.z)

    def sibling(self):
        return self.dev(self.x, self.y, 1 - self.c, self.z)

    def blk(self, d1, d2):
        x, y = self.xy(d1, d2)
        return ((y % 2) * 2 + self.c) * 8 + (y // 2) * 4 + x

    def zpeer(self, d):
        return self.dev(self.x, self.y, self.c, (self.z + d + 4) % 4)

    def sp_peer(self, k):
        return (self.f, (self.s + k) % 8, self.z)


def barrier(devices):
    sem = pltpu.get_barrier_semaphore()
    for d in devices:
        pl.semaphore_signal(sem, inc=1, device_id=d, device_id_type=MESH)
    pl.semaphore_wait(sem, len(devices))


def remote(src, dst, send, recv, device):
    pltpu.make_async_remote_copy(
        src_ref=src, dst_ref=dst, send_sem=send, recv_sem=recv, device_id=device, device_id_type=MESH
    ).start()


def wait_bytes(ref, sem):
    pltpu.make_async_copy(ref, ref, sem).wait()


STEP = (0, -1, 1, 2)


class Gather:
    def __init__(self, p, shard, w, send, recv, local):
        self.p, self.shard, self.w, self.send, self.recv, self.local = p, shard, w, send, recv, local

    def push(self, b, sem, device, half=None, src=None):
        dst = self.w.at[b] if half is None else self.w.at[b, pl.ds(32 * half, 32)]
        remote(dst if src is None else src, dst, self.send, self.recv.at[sem], device)

    def arrive(self, b, sem):
        wait_bytes(self.w.at[b], self.recv.at[sem])

    def start(self):
        p, s = self.p, self.shard
        own = p.blk(0, 0)
        for sem, device in ((0, p.peer(1, 0)), (1, p.peer(-1, 0)), (3, p.peer(0, 1)), (7, p.peer(0, -1)), (15, p.sibling())):
            self.push(own, sem, device, src=s)
        pltpu.make_async_copy(s, self.w.at[own], self.local).start()

    def second(self, j):
        p = self.p
        b = p.blk(STEP[j], 0)
        self.push(b, 3 + j, p.peer(0, 1))
        self.push(b, 7 + j, p.peer(0, -1))
        self.push(b, 15, p.sibling())

    def first_low(self):
        p = self.p
        b = p.blk(-1, 0)
        self.arrive(b, 0)
        self.push(b, 2, p.peer(1, 0), half=0)
        self.second(1)

    def first_high(self):
        p = self.p
        b = p.blk(1, 0)
        self.arrive(b, 1)
        self.push(b, 2, p.peer(-1, 0), half=1)
        self.second(2)

    def first_far(self):
        self.arrive(self.p.blk(2, 0), 2)
        self.second(3)

    def low(self, j):
        p = self.p
        b = p.blk(STEP[j], -1)
        self.arrive(b, 3 + j)
        self.push(b, 11 + j, p.peer(0, 1), half=0)
        self.push(b, 15, p.sibling())

    def high(self, j):
        p = self.p
        b = p.blk(STEP[j], 1)
        self.arrive(b, 7 + j)
        self.push(b, 11 + j, p.peer(0, -1), half=1)
        self.push(b, 15, p.sibling())

    def far(self, j):
        b = self.p.blk(STEP[j], 2)
        self.arrive(b, 11 + j)
        self.push(b, 15, self.p.sibling())

    def end(self):
        wait_bytes(self.w.at[pl.ds(0, 16)], self.recv.at[15])
        own = self.p.blk(0, 0)
        pltpu.make_async_copy(self.shard, self.w.at[own], self.local).wait()

    def drain(self):
        wait_bytes(self.w.at[pl.ds(0, 31)], self.send)

    def ticks(self):
        part = functools.partial
        return [
            self.first_low, self.first_high, part(self.low, 0), part(self.high, 0), self.first_far,
            part(self.low, 1), part(self.high, 1), part(self.far, 0), part(self.low, 2), part(self.high, 2), part(self.far, 1),
            part(self.low, 3), part(self.high, 3), part(self.far, 2), part(self.far, 3), self.end,
        ]


class Ticks:
    def __init__(self):
        self.todo, self.now = [], 0.0

    def add(self, time, fn):
        self.todo.append((time, len(self.todo), fn))
        self.todo.sort(key=lambda e: e[:2])

    def series(self, first, step, fns):
        for k, fn in enumerate(fns):
            self.add(first + k * step, fn)

    def serve(self):
        while self.todo and self.todo[0][0] <= self.now:
            self.todo.pop(0)[2]()

    def step(self, us):
        self.now += us
        self.serve()

    def until_time(self, time):
        self.now = max(self.now, time)
        self.serve()

    def until(self, fn):
        for time, _, f in self.todo:
            if f == fn:
                self.now = max(self.now, time)
        self.serve()


ATT = dict(
    q=((2048, 64), BF), k=((2048, 64), BF), v=((2048, 64), BF), g=((2048, 64), BF),
    kt=((64, 2048), BF), vt=((80, 2048), BF), gt=((64, 2048), F32),
    dkv=((2048, 128), F32), mx=((8, TQ), F32), st=((4, TQ, TQ), F32), e=((4, TQ, TQ), BF),
    ot=((80, TQ), F32), dq=((64, TQ), F32), g2=((TQ, 64), BF),
)


def split_heads(recv, seq, b):
    @pl.loop(0, 8)
    def _(i):
        part = recv[i, pl.ds(seq * 256, 256), :]
        rows = pl.ds(i * 256, 256)
        q, k, v, g = (part[:, 64 * n : 64 * n + 64] for n in range(4))
        b.q[rows, :] = q
        b.k[rows, :] = k
        b.v[rows, :] = v
        b.g[rows, :] = g
        cols = pl.ds(pl.multiple_of(i * 256, 256), 256)
        b.kt[:, cols] = k.astype(F32).T.astype(BF)
        b.vt[0:64, cols] = v.astype(F32).T.astype(BF)
        b.gt[:, cols] = g.astype(F32).T

    b.vt[64:80, :] = jnp.ones((16, 2048), BF)
    b.dkv[...] = jnp.zeros(b.dkv.shape, F32)


def attend_block(qi, seq, b, send, ticks):
    scale = 0.125 * LOG2E
    qrows = slice(qi * TQ, (qi + 1) * TQ)
    q = b.q[qrows, :]
    b.mx[...] = jnp.full((8, TQ), -1e30, F32)
    for j in range(qi + 1):
        st = dot_nt(b.k[j * TQ : (j + 1) * TQ, :], q)
        if j == qi:
            key = lax.broadcasted_iota(jnp.int32, (TQ, TQ), 0)
            query = lax.broadcasted_iota(jnp.int32, (TQ, TQ), 1)
            st = jnp.where(key <= query, st, -1e30)
        b.st[j] = st
        b.mx[...] = jnp.maximum(b.mx[...], jnp.max(st.reshape(TQ // 8, 8, TQ), axis=0))
        ticks.step(0.45)
    top = jnp.max(b.mx[...], axis=0, keepdims=True) * scale
    b.ot[...] = jnp.zeros(b.ot.shape, F32)
    for j in range(qi + 1):
        e = jnp.exp2(b.st[j] * scale - top).astype(BF)
        b.e[j] = e
        b.ot[...] += dot_nn(b.vt[:, j * TQ : (j + 1) * TQ], e)
        ticks.step(0.45)
    inv = 1.0 / b.ot[64:65, :]
    out = b.ot[0:64, :] * inv
    gt = b.gt[:, qrows] * inv
    inner = jnp.sum(out * gt, axis=0, keepdims=True)
    b.g2[...] = gt.T.astype(BF)
    b.dq[...] = jnp.zeros(b.dq.shape, F32)
    for j in range(qi + 1):
        rows = slice(j * TQ, (j + 1) * TQ)
        g2 = b.g2[...]
        dp = dot_nt(b.v[rows, :], g2)
        e = b.e[j]
        ds = (e.astype(F32) * (dp - inner)).astype(BF)
        b.dkv[rows, 0:64] += dot_nn(ds, b.q[qrows, :])
        b.dkv[rows, 64:128] += dot_nn(e, g2)
        b.dq[...] += dot_nn(b.kt[:, j * TQ : (j + 1) * TQ], ds)
        ticks.step(0.9)
    both = jnp.concatenate([out, b.dq[...] * 0.125], axis=0).T.astype(BF)
    for h in range(2):
        send[qi * 2 + h, seq * 256 : (seq + 1) * 256, 0:128] = both[h * 256 : (h + 1) * 256]


def finish_heads(seq, b, send):
    @pl.loop(0, 8)
    def _(i):
        t = b.dkv[pl.ds(i * 256, 256), :]
        lane = lax.broadcasted_iota(jnp.int32, t.shape, 1)
        send[i, pl.ds(seq * 256, 256), 128:256] = (t * jnp.where(lane < 64, 0.125, 1.0)).astype(BF)


def turn(a, cos, low, high):
    return a * cos + pltpu.roll(a, 112, 1) * low + pltpu.roll(a, 16, 1) * high


FAR_FIRST = (2, 1, -1, 0)


class Scatter:
    def __init__(self, p, product, r, sbuf, rest, ssend, srecv, send, recv):
        self.p, self.product, self.r, self.sbuf = p, product, r, sbuf
        self.half, self.full = (lambda j, h: rest(j, 32 * h, 32)), (lambda j, h: rest(4 + 2 * j + h, 0, 64))
        self.half1, self.full1 = (lambda h: rest(12, 32 * h, 32)), (lambda h: rest(13 + h, 0, 64))
        self.ssend, self.srecv, self.send, self.recv = ssend, srecv, send, recv

    def group(self, d):
        y = (self.p.y + d + 4) % 4
        return (y % 2) * 2 + y // 2

    def rb(self, d1, d2):
        x, y = self.p.xy(d1, d2)
        return ((y % 2) * 2 + y // 2) * 4 + x

    def hand_over(self, n):
        k = self.group(FAR_FIRST[n])
        blocks = pl.ds(k * 4, 4)

        def store(cols, value):
            self.sbuf[blocks, :, cols] = value.astype(BF).reshape(4, 64, value.shape[1])

        self.product(k, 1 - self.p.c, store)
        remote(self.sbuf.at[blocks], self.r.at[blocks], self.ssend, self.srecv.at[n], self.p.sibling())

    def handed_over(self):
        wait_bytes(self.sbuf, self.ssend)

    def own_group(self, n):
        k = self.group(FAR_FIRST[n])
        blocks = pl.ds(k * 4, 4)
        wait_bytes(self.r.at[blocks], self.srecv.at[n])

        def store(cols, value):
            total = value.reshape(4, 64, value.shape[1]) + self.r[blocks, :, cols].astype(F32)
            self.r[blocks, :, cols] = total.astype(BF)

        self.product(k, self.p.c, store)

    def add(self, dst, src):
        dst[...] = (dst[...].astype(F32) + src[...].astype(F32)).astype(BF)

    def rows(self, d1, d2, h):
        return self.r.at[self.rb(d1, d2), pl.ds(32 * h, 32)]

    def far(self, j):
        p, d = self.p, FAR_FIRST[j]
        for h, to in ((0, 1), (1, -1)):
            remote(self.rows(d, 2, h), self.half(j, h), self.send, self.recv.at[2 * j + h], p.peer(0, to))

    def near(self, j):
        p, d = self.p, FAR_FIRST[j]
        for h, to in ((0, 1), (1, -1)):
            wait_bytes(self.half(j, h), self.recv.at[2 * j + h])
            self.add(self.rows(d, to, h), self.half(j, h))
            remote(self.r.at[self.rb(d, to)], self.full(j, h), self.send, self.recv.at[8 + 2 * j + h], p.peer(0, to))

    def sum(self, j):
        for h in range(2):
            wait_bytes(self.full(j, h), self.recv.at[8 + 2 * j + h])
        dst = self.r.at[self.rb(FAR_FIRST[j], 0)]
        dst[...] = (dst[...].astype(F32) + self.full(j, 0)[...].astype(F32) + self.full(j, 1)[...].astype(F32)).astype(BF)

    def far1(self):
        for h, to in ((0, 1), (1, -1)):
            remote(self.rows(2, 0, h), self.half1(h), self.send, self.recv.at[16 + h], self.p.peer(to, 0))

    def near1(self):
        for h, to in ((0, 1), (1, -1)):
            wait_bytes(self.half1(h), self.recv.at[16 + h])
            self.add(self.rows(to, 0, h), self.half1(h))
            remote(self.r.at[self.rb(to, 0)], self.full1(h), self.send, self.recv.at[18 + h], self.p.peer(to, 0))

    def sum1(self, out):
        for h in range(2):
            wait_bytes(self.full1(h), self.recv.at[18 + h])
        out[...] = self.r[self.rb(0, 0)].astype(F32) + self.full1(0)[...].astype(F32) + self.full1(1)[...].astype(F32)

    def drain(self):
        wait_bytes(self.r.at[pl.ds(0, 15)], self.send)


class Depth:
    def __init__(self, p, a, half, full, rsend, gsend, recv, spare, one):
        self.p, self.a, self.half, self.full, self.spare, self.one = p, a, half, full, spare, one
        self.rsend, self.gsend, self.recv = rsend, gsend, recv

    def rows(self, ref, d, h=None):
        z = (self.p.z + d + 4) % 4
        return ref.at[pl.ds(z * 128, 128)] if h is None else ref.at[pl.ds(z * 128 + 64 * h, 64)]

    def far(self):
        for h, to in ((0, 1), (1, -1)):
            remote(self.rows(self.a, 2, h), self.half.at[h], self.rsend, self.recv.at[h], self.p.zpeer(to))

    def near(self):
        for h, to in ((0, 1), (1, -1)):
            wait_bytes(self.half.at[h], self.recv.at[h])
            dst = self.rows(self.a, to, h)
            dst[...] = (dst[...].astype(F32) + self.half[h].astype(F32)).astype(BF)
            remote(self.rows(self.a, to), self.full.at[h], self.rsend, self.recv.at[2 + h], self.p.zpeer(to))

    def release(self):
        wait_bytes(self.a.at[pl.ds(0, 384)], self.rsend)
        for to in (1, -1):
            pl.semaphore_signal(self.spare, inc=self.one, device_id=self.p.zpeer(to), device_id_type=MESH)

    def arrived(self):
        for h in range(2):
            wait_bytes(self.full.at[h], self.recv.at[2 + h])

    def total(self, r):
        own = self.a[pl.ds(self.p.z * 128 + r, 32), :].astype(F32)
        return own + self.full[0, pl.ds(r, 32), :].astype(F32) + self.full[1, pl.ds(r, 32), :].astype(F32)

    def give(self):
        pl.semaphore_wait(self.spare, self.one * 2)
        src = self.rows(self.a, 0)
        for h, to in ((0, 1), (1, -1)):
            remote(src, src, self.gsend, self.recv.at[4 + h], self.p.zpeer(to))

    def give_on(self):
        for h, to in ((0, 1), (1, -1)):
            wait_bytes(self.rows(self.a, -to), self.recv.at[4 + h])
            src = self.rows(self.a, -to, h)
            remote(src, src, self.gsend, self.recv.at[6], self.p.zpeer(to))

    def given(self):
        wait_bytes(self.rows(self.a, 2), self.recv.at[6])

    def drain(self):
        wait_bytes(self.a.at[pl.ds(0, 384)], self.gsend)


K1 = dict(
    wa=((32, 64, 2048), BF), wb=((32, 64, 2048), BF), wc=((32, 64, 2048), BF),
    hid=((512, 2048), BF), gv=((512, 2048), BF), act=((512, 2048), BF), din=((512, 2048), BF),
    hs=((8, 512, 256), BF), hr=((8, 512, 256), BF), br=((8, 512, 256), BF), gp=((512, 2048), BF),
    dproj=((512, 1536), BF), att=((512, 512), BF), sums=((8, 2048), F32), sa=((64, 2048), BF),
    cos=((256, 128), F32), low=((256, 128), F32), high=((256, 128), F32),
)
LATE = dict(
    rc=((47, 64, 2048), BF), zh=((2, 2, 64, 2048), BF), zf=((2, 2, 128, 2048), BF), xr=((128, 2048), BF), gr=((128, 2048), BF),
    res=((64, 2048), F32), vec=((5, 8, 2048), F32), vin=((10, 8, 2048), F32),
)

SERVE_A = (6.0, 1.7)
START_B = 24.0
SERVE_B = (38.0, 2.4)
START_C = 62.0
SERVE_C = (72.0, 2.9)
HEADS_IN = 58.0


def block_kernel(
    x_hbm, g_hbm, wq, wd, sb, sc, prm, bqkv,
    o_mixed, o_tok, o_res, o_vec, o_ht, o_gt, *refs,
):
    m = Scratch(K1, refs[: len(K1)])
    (
        wsend, wrecv, wlocal, asend, arecv, local, lout, ssend, srecv, send, recv, zrs, zgs, zrecv, vsend, vrecv, here, free, spare,
    ) = refs[len(K1) :]
    p = Place()
    pieces = [pltpu.make_async_copy(wq.at[n], m.sa.at[:, n * 512 : n * 512 + 512], local.at[0]) for n in range(3)]
    pieces.append(pltpu.make_async_copy(wd, m.sa.at[:, 1536:2048], local.at[0]))
    for c in pieces:
        c.start()
    shard = pltpu.make_async_copy(m.sa, m.sa, local.at[0])
    xs = [p.dev((p.x + k) % 4, p.y, p.c, p.z) for k in (1, 2, 3)]
    ys = [p.dev(p.x, (p.y + k) % 4, p.c, p.z) for k in (1, 2, 3)]
    zs = [p.zpeer(k) for k in (1, 2, 3)]
    far = [p.dev((p.x + k) % 4, (p.y + 2) % 4, p.c, p.z) for k in (1, 2, 3)]
    barrier(xs + ys + zs + far + [p.sibling()])
    near = [xs[0], xs[2], ys[0], ys[2], zs[0], zs[2], p.sibling()]

    one = p.z * 0 + 1
    seven = one * 7

    def say(sem):
        for d in near:
            pl.semaphore_signal(sem, inc=one, device_id=d, device_id_type=MESH)

    ga, gb, gc = (
        Gather(p, s, w, wsend.at[i], wrecv.at[i], wlocal.at[i]) for i, (s, w) in enumerate(((m.sa, m.wa), (sb, m.wb), (sc, m.wc)))
    )
    shard.wait()
    ga.start()
    load_x = pltpu.make_async_copy(x_hbm, m.act, local.at[0])
    load_g = pltpu.make_async_copy(g_hbm, m.gv, local.at[1])
    load_x.start()
    load_g.start()
    ticks = Ticks()
    ticks.series(*SERVE_A, ga.ticks())
    ticks.add(START_B, gb.start)
    ticks.series(*SERVE_B, gb.ticks())
    ticks.add(START_C, gc.start)
    ticks.series(*SERVE_C, gc.ticks())

    lane = lax.broadcasted_iota(jnp.int32, (256, 128), 1) % 64
    place = (p.s * 256 + lax.broadcasted_iota(jnp.int32, (256, 128), 0)).astype(F32)
    angle = place * jnp.exp((lane % 16).astype(F32) * (-2.0 * math.log(10000.0) / ROT))
    sine = jnp.sin(angle)
    m.cos[...] = jnp.where(lane < 32, jnp.cos(angle), 1.0)
    m.low[...] = jnp.where(lane < 16, -sine, 0.0)
    m.high[...] = jnp.where((lane >= 16) & (lane < 32), sine, 0.0)
    cos, low, high = m.cos, m.low, m.high
    gain, shift, bfc1 = prm.at[0:1], prm.at[1:2], prm.at[3:4]
    load_x.wait()

    def norm_rows(n):
        @pl.loop(0, 4)
        def _(r):
            rows = pl.ds(n * 128 + r * 32, 32)
            x = m.act[rows, :].astype(F32)
            cent = x - jnp.mean(x, axis=-1, keepdims=True)
            inv = lax.rsqrt(jnp.mean(cent * cent, axis=-1, keepdims=True) + 1e-05)
            m.hid[rows, :] = (cent * inv * gain[...] + shift[...]).astype(BF)

    for n in range(4):
        norm_rows(n)
        ticks.step(0.9)
    outs = []

    def put(src, dst):
        c = pltpu.make_async_copy(src, dst, lout.at[len(outs)])
        c.start()
        outs.append(c)

    load_g.wait()

    def flip(src, dst, n):
        at, half = n // 2, n % 2
        dst[at * 2 + half] = src[half * 256 : half * 256 + 256, at * 512 : at * 512 + 512].astype(F32).T.astype(BF)

    for n in range(8):
        flip(m.gv, m.hs, n)
        ticks.step(0.4)
    put(m.hs, o_gt)
    for n in range(8):
        flip(m.hid, m.br, n)
        ticks.step(0.4)
    put(m.br, o_ht)

    @pl.loop(0, 8)
    def _(n):
        cols = pl.ds(pl.multiple_of(n * 256, 256), 256)
        m.sums[2:3, cols] = jnp.sum(m.gv[:, cols].astype(F32), axis=0, keepdims=True)

    ticks.until(ga.end)

    outs[0].wait()
    outs[1].wait()

    for part in range(4):
        for t in range(2):
            col = part * 512 + t * 256
            lhs = m.gv if part == 3 else m.hid
            acc = dot_nn(lhs[...], m.wa[:, :, col : col + 256].reshape(2048, 256))
            if part < 3:
                acc = acc + bqkv[part : part + 1, t * 256 : t * 256 + 256]
            for sq in range(2):
                for lh in range(2):
                    a = acc[sq * 256 : (sq + 1) * 256, lh * 128 : (lh + 1) * 128]
                    if part < 2:
                        a = turn(a, cos[...], low[...], high[...])
                    a = a.astype(BF)
                    for e in range(2):
                        m.hs[t * 4 + lh * 2 + e, sq * 256 : (sq + 1) * 256, part * 64 : part * 64 + 64] = a[:, e * 64 : e * 64 + 64]
            ticks.step(0.75)

    def exchange(dst, recv, seq, base):
        rows = pl.ds(seq * 256, 256)
        for k in range(1, 8):
            to = (p.s + k) % 8
            remote(m.hs.at[to, rows], dst.at[p.s, rows], asend.at[base], recv, p.sp_peer(k))
        pltpu.make_async_copy(m.hs.at[p.s, rows], dst.at[p.s, rows], local.at[2 + base]).start()

    def exchanged(dst, recv, seq, base):
        rows = pl.ds(seq * 256, 256)
        wait_bytes(dst.at[pl.ds(0, 7), rows], recv)
        pltpu.make_async_copy(m.hs.at[p.s, rows], dst.at[p.s, rows], local.at[2 + base]).wait()

    def sent(base):
        wait_bytes(m.hs.at[pl.ds(0, 7), pl.ds(0, 256)], asend.at[base])

    for seq in range(2):
        exchange(m.hr, arecv.at[seq], seq, seq)
    ticks.step(1.0)
    ticks.until_time(HEADS_IN)


    def heads(*scratch):
        b = Scratch(ATT, scratch)
        for seq in range(2):
            exchanged(m.hr, arecv.at[seq], seq, seq)
            split_heads(m.hr, seq, b)
            ticks.step(1.5)
            if seq == 0:
                sent(0)
                sent(1)
            for qi in range(4):
                attend_block(qi, seq, b, m.hs, ticks)
            finish_heads(seq, b, m.hs)
            ticks.step(0.7)
            exchange(m.br, arecv.at[2 + seq], seq, 2 + seq)

    pl.run_scoped(heads, *[pltpu.VMEM(*v) for v in ATT.values()])
    load_gt = pltpu.make_async_copy(o_gt, m.hr, local.at[0])
    load_gt.start()

    def hidden_units(n):
        cols = slice(n * 256, n * 256 + 256)
        u = dot_nn(m.hid[...], m.wb[:, :, cols].reshape(2048, 256)) + bfc1[:, cols]
        k = math.sqrt(2.0 / math.pi)
        sq = u * u
        th = jnp.tanh(u * (k + (k * 0.044715) * sq))
        half = 0.5 + 0.5 * th
        m.act[:, cols] = (u * half).astype(BF)
        m.gp[:, cols] = (half + (0.5 * u) * (1.0 - th * th) * (k + (3.0 * k * 0.044715) * sq)).astype(BF)

    ticks.until(gb.end)
    for n in range(8):
        hidden_units(n)
        ticks.step(0.9)

    def late(*scratch):
        b = Scratch(LATE, scratch)
        say(here)
        zrow = pl.ds(p.z * 128, 128)
        loads = [pltpu.make_async_copy(s.at[zrow], d, local.at[6 + i]) for i, (s, d) in enumerate(((x_hbm, b.xr), (g_hbm, b.gr)))]
        for c in loads:
            c.start()
        finish(b, loads)

    def finish(b, loads):
        def product(pairs):
            def run(k, cc, store):
                def tile(left, right, col, dst):
                    rows = pl.ds((k % 2) * 256, 256)
                    at = ((k // 2) * 2 + cc) * 2
                    lhs0, lhs1 = left[at, rows, :], left[at + 1, rows, :]
                    store(dst, dot_nn(lhs0, right[0:256, col]) + dot_nn(lhs1, right[256:512, col]))

                for left, right, start, count in pairs:

                    @pl.loop(0, count)
                    def _(t):
                        tile(left, right, pl.ds(pl.multiple_of(t * 512, 512), 512), pl.ds(pl.multiple_of(start + t * 512, 512), 512))

            return run

        pairs = ([(m.hr, m.act, 0, 4)], [(m.hs, m.din, 0, 4)], [(m.hs, m.dproj, 0, 3), (m.hr, m.att, 1536, 1)])

        def rows_of(ref, base):
            return lambda n, start, count: ref.at[base + n, pl.ds(start, count)]

        spaces = (
            (b.rc.at[pl.ds(0, 16)], b.rc.at[pl.ds(16, 16)], rows_of(b.rc, 32)),
            (m.wb.at[pl.ds(0, 16)], m.wb.at[pl.ds(16, 16)], rows_of(m.wc, 0)),
            (m.wa.at[pl.ds(0, 16)], m.wa.at[pl.ds(16, 16)], rows_of(m.wc, 15)),
        )
        sc = [Scatter(p, product(pairs[i]), *spaces[i], ssend.at[i], srecv.at[i], send.at[i], recv.at[i]) for i in range(3)]
        zn, zm = (Depth(p, a, b.zh.at[i], b.zf.at[i], zrs.at[i], zgs.at[i], zrecv.at[i], spare.at[i], one) for i, a in enumerate((m.hid, m.gv)))
        v = b.vec.at[0]
        gain, bout = prm.at[0:1], prm.at[2:3]

        def norm_back(i):
            r = i * 32
            x32 = b.xr[pl.ds(r, 32), :].astype(F32)
            cent = x32 - jnp.mean(x32, axis=-1, keepdims=True)
            inv = lax.rsqrt(jnp.mean(cent * cent, axis=-1, keepdims=True) + 1e-05)
            xn = cent * inv
            gn = zn.total(r)
            v[0:1, :] += jnp.sum(gn * xn, axis=0, keepdims=True)
            v[1:2, :] += jnp.sum(gn, axis=0, keepdims=True)
            gn = gn * gain[...]
            gx = inv * (gn - jnp.mean(gn, axis=-1, keepdims=True) - xn * jnp.mean(gn * xn, axis=-1, keepdims=True))
            m.hid[pl.ds(p.z * 128 + r, 32), :] = (b.gr[pl.ds(r, 32), :].astype(F32) + gx).astype(BF)

        def vsends(stage, peers, base):
            for i, d in enumerate(peers):
                remote(b.vec.at[stage], b.vin.at[base + i], vsend, vrecv.at[base + i], d)

        def vsum(stage, count, base, rows):
            total = b.vec[stage]
            for i in range(count):
                wait_bytes(b.vin.at[base + i], vrecv.at[base + i])
                part = b.vin[base + i]
                if rows < 8:
                    part = jnp.where(lax.broadcasted_iota(jnp.int32, part.shape, 0) < rows, part, 0.0)
                total = total + part
            b.vec[stage + 1] = total

        def hand(i, n):
            sc[i].hand_over(n)

        def own(i, n):
            sc[i].own_group(n)
            sc[i].far(n)

        def last(i):
            if i > 0:
                wait_bytes(b.res, local.at[0])
            sc[i].sum1(b.res)
            pltpu.make_async_copy(b.res, o_res.at[i], local.at[0]).start()

        v[...] = jnp.zeros((8, 2048), F32)
        load_gt.wait()
        pl.semaphore_wait(here, seven)
        for n in range(4):
            hand(0, n)
        ticks.until(gc.end)
        for n in range(8):
            cols = slice(n * 256, n * 256 + 256)
            ga_ = dot_nn(m.gv[...], m.wc[:, :, cols].reshape(2048, 256))
            d = (ga_ * m.gp[:, cols].astype(F32)).astype(BF)
            m.din[:, cols] = d
            m.sums[0:1, cols] = jnp.sum(d.astype(F32), axis=0, keepdims=True)
            if n % 2:
                own(0, n // 2)
        for g in (ga, gb, gc):
            g.drain()
        for seq in range(2):
            exchanged(m.br, arecv.at[2 + seq], seq, 2 + seq)
        sent(2)
        sent(3)
        load_ht = pltpu.make_async_copy(o_ht, m.hs, local.at[1])
        load_ht.start()

        for hp in range(4):
            pair = [m.br[2 * hp + e] for e in range(2)]
            for n in range(4):
                a = jnp.concatenate([pair[e][:, n * 64 : n * 64 + 64] for e in range(2)], axis=1)
                cols = slice(hp * 128, hp * 128 + 128)
                if n == 0:
                    m.att[:, cols] = a
                    continue
                if n < 3:
                    a = a.astype(F32)
                    a = jnp.concatenate(
                        [turn(a[sq * 256 : sq * 256 + 256], cos[...], -low[...], -high[...]) for sq in range(2)], axis=0
                    ).astype(BF)
                cols = slice((n - 1) * 512 + hp * 128, (n - 1) * 512 + hp * 128 + 128)
                m.dproj[:, cols] = a
                m.sums[1:2, cols] = jnp.sum(a.astype(F32), axis=0, keepdims=True)

        sc[0].near(0)
        sc[0].near(1)

        @pl.loop(0, 4)
        def _(t):
            rows = pl.ds(t * 8, 8)
            cols = pl.ds(pl.multiple_of(t * 512, 512), 512)
            norm = dot_nt(m.dproj[...], m.wa[rows, :, 0:1536].reshape(512, 1536))
            norm = norm + dot_nt(m.din[...], m.wb[rows].reshape(512, 2048))
            m.hid[:, cols] = norm.astype(BF)

        zn.far()
        sc[0].near(2)
        sc[0].near(3)

        @pl.loop(0, 4)
        def _(t):
            rows = pl.ds(t * 8, 8)
            cols = pl.ds(pl.multiple_of(t * 512, 512), 512)
            mixed = dot_nt(m.att[...], m.wa[rows, :, 1536:2048].reshape(512, 512))
            mixed = mixed + dot_nt(m.act[...], m.wc[rows].reshape(512, 2048))
            m.gv[:, cols] = mixed.astype(BF)

        say(free)
        zn.near()
        zm.far()
        load_ht.wait()
        pl.semaphore_wait(free, seven)
        for n in range(4):
            hand(1, n)
        sc[0].sum(0)
        sc[0].far1()
        for n in range(4):
            hand(2, n)
        own(1, 0)
        own(1, 1)
        sc[0].sum(1)
        sc[0].sum(2)
        sc[0].near1()
        own(1, 2)
        own(1, 3)
        for c in loads:
            c.wait()
        zn.arrived()
        zn.release()

        @pl.loop(0, 4)
        def _(i):
            norm_back(i)

        zn.give()
        v[2:3, :] = m.sums[2:3, :]
        v[3:4, :] = m.sums[0:1, :]
        v[4:5, :] = m.sums[1:2, :]
        vsends(0, zs, 0)
        sc[1].near(0)
        sc[1].near(1)
        own(2, 0)
        own(2, 1)
        zm.near()
        sc[1].near(2)
        sc[1].near(3)
        own(2, 2)
        own(2, 3)
        sc[0].sum(3)
        last(0)
        vsum(0, 3, 0, 2)
        vsends(1, ys, 3)
        sc[1].sum(0)
        sc[1].far1()
        zn.give_on()
        sc[2].near(0)
        sc[2].near(1)
        zm.arrived()
        zm.release()

        @pl.loop(0, 4)
        def _(i):
            r = i * 32
            total = zm.total(r) + b.xr[pl.ds(r, 32), :].astype(F32) + bout[...]
            m.gv[pl.ds(p.z * 128 + r, 32), :] = total.astype(BF)

        zm.give()
        sc[1].sum(1)
        sc[1].sum(2)
        sc[1].near1()
        sc[2].near(2)
        sc[2].near(3)
        vsum(1, 3, 3, 8)
        vsends(2, xs, 6)
        sc[1].sum(3)
        sc[2].sum(0)
        sc[2].far1()
        last(1)
        zm.give_on()
        sc[2].sum(1)
        sc[2].sum(2)
        sc[2].near1()
        vsum(2, 3, 6, 8)
        vsends(3, [p.sibling()], 9)
        zn.given()
        put(m.hid, o_tok)
        sc[2].sum(3)
        zm.given()
        put(m.gv, o_mixed)
        vsum(3, 1, 9, 8)
        put(b.vec.at[4], o_vec)
        last(2)
        wait_bytes(b.res, local.at[0])
        for s in sc:
            s.drain()
            s.handed_over()
        zn.drain()
        zm.drain()
        wait_bytes(b.vin, vsend)
        for c in outs[2:]:
            c.wait()

    pl.run_scoped(late, *[pltpu.VMEM(*v) for v in LATE.values()])


def run_block(x, g, wq, wd, sb, sc, prm, bqkv):
    hbm = pl.BlockSpec(memory_space=pl.ANY)
    vmem = pl.BlockSpec(memory_space=pltpu.VMEM)
    full = jax.ShapeDtypeStruct((512, 2048), BF)
    flipped = jax.ShapeDtypeStruct((8, 512, 256), BF)
    dma, plain = pltpu.SemaphoreType.DMA, pltpu.SemaphoreType.REGULAR
    return pl.pallas_call(
        block_kernel,
        out_shape=[full, full, jax.ShapeDtypeStruct((3, 64, 2048), F32), jax.ShapeDtypeStruct((8, 2048), F32), flipped, flipped],
        in_specs=[hbm] * 6 + [vmem] * 2,
        out_specs=[hbm] * 6,
        scratch_shapes=[pltpu.VMEM(*v) for v in K1.values()]
        + [dma((3,)), dma((3, 16)), dma((3,)), dma((4,)), dma((4,)), dma((8,)), dma((8,))]
        + [dma((3,)), dma((3, 4)), dma((3,)), dma((3, 20)), dma((2,)), dma((2,)), dma((2, 7)), dma(()), dma((10,)), plain, plain, plain((2,))],
        compiler_params=pltpu.CompilerParams(collective_id=0, has_side_effects=True, vmem_limit_bytes=62 * MIB),
        cost_estimate=pl.CostEstimate(flops=43 * 10**9, bytes_accessed=30 * 10**6, transcendentals=10**7),
    )(x, g, wq, wd, sb, sc, prm, bqkv)


def place_kernel(mixed, tok, res, vec, o_mixed, o_tok, gq, gd, g1, g2, gain, shift, bq, bo, b1, bo2, *scratch):
    a, b, r, come, go = scratch
    loads = [pltpu.make_async_copy(s, d, come.at[i]) for i, (s, d) in enumerate(((mixed, a), (tok, b), (res, r)))]
    for c in loads:
        c.start()
    for row, out in ((0, gain), (1, shift), (2, bo), (2, bo2), (3, b1)):
        out[...] = vec[row : row + 1, :]
    for n in range(3):
        bq[n : n + 1, :] = vec[4:5, n * 512 : n * 512 + 512]
    moves = [(a, o_mixed, 0), (b, o_tok, 1), (r.at[1], g1, 2), (r.at[0], g2, 2), (r.at[2, :, pl.ds(1536, 512)], gd, 2)]
    moves += [(r.at[2, :, pl.ds(n * 512, 512)], gq.at[n], 2) for n in range(3)]
    copies = [pltpu.make_async_copy(s, d, go.at[i]) for i, (s, d, _) in enumerate(moves)]
    for i, c in enumerate(loads):
        c.wait()
        for move, copy in zip(moves, copies):
            if move[2] == i:
                copy.start()
    for c in copies:
        c.wait()


def place_outputs(mixed, tok, res, vec):
    hbm = pl.BlockSpec(memory_space=pl.ANY)
    vmem = pl.BlockSpec(memory_space=pltpu.VMEM)
    full = jax.ShapeDtypeStruct((512, 2048), BF)

    def f32(*shape):
        return jax.ShapeDtypeStruct(shape, F32)

    row = f32(1, 2048)
    dma = pltpu.SemaphoreType.DMA
    return pl.pallas_call(
        place_kernel,
        out_shape=[full, full, f32(3, 64, 512), f32(64, 512), f32(64, 2048), f32(64, 2048), row, row, f32(3, 512), row, row, row],
        in_specs=[hbm] * 3 + [vmem],
        out_specs=[hbm] * 6 + [vmem] * 6,
        scratch_shapes=[pltpu.VMEM((512, 2048), BF)] * 2 + [pltpu.VMEM((3, 64, 2048), F32), dma((3,)), dma((8,))],
        compiler_params=pltpu.CompilerParams(vmem_limit_bytes=60 * MIB),
    )(mixed, tok, res, vec)


def body(tokens, ln_gain, ln_bias, w_qkv, b_qkv, w_dense, b_dense, w_fc1, b_fc1, w_fc2, b_fc2, cotangent):
    width = tokens.shape[2]
    x = tokens.reshape(-1, width)
    g = cotangent.reshape(-1, width)
    zero = jnp.zeros((width,), F32)
    prm = jnp.stack(
        [ln_gain.astype(F32), ln_bias.astype(F32), b_dense.astype(F32) + b_fc2.astype(F32), b_fc1.astype(F32)] + [zero] * 4
    )
    mixed_out, grad_tokens, res, vec, _, _ = run_block(
        x, g, w_qkv.transpose(1, 0, 2), w_dense.T, w_fc1, w_fc2.T, prm, b_qkv.astype(F32)
    )
    mixed_out, grad_tokens, gq, gd, g1, g2, gain, shift, bq, bo, b1, bo2 = place_outputs(mixed_out, grad_tokens, res, vec)
    return (
        mixed_out.reshape(tokens.shape), grad_tokens.reshape(tokens.shape), gain[0], shift[0], gq.transpose(1, 0, 2), bq, gd.T,
        bo[0], g1, b1[0], g2.T, bo2[0],
    )


def solution(mesh):
    both = ("fsdp", "sp")
    act = P("fsdp", "sp", None)
    in_specs = (
        act, P(), P(), P(both, None, "tp"), P(None, "tp"), P("tp", both), P(), P(both, "tp"), P("tp"), P("tp", both), P(), act,
    )
    out_specs = (
        act, act, P(), P(), P(both, None, "tp"), P(None, "tp"), P("tp", both), P(), P(both, "tp"), P("tp"), P("tp", both), P(),
    )
    return jax.shard_map(body, mesh=mesh, in_specs=in_specs, out_specs=out_specs, check_vma=False)
```

```python
import functools
import math

import jax
import jax.numpy as jnp
from jax import lax
from jax.experimental import pallas as pl
from jax.experimental.pallas import tpu as pltpu
from jax.sharding import PartitionSpec as P

MESH = pl.DeviceIdType.MESH
F32 = jnp.float32
BF = jnp.bfloat16
HDIM = 64
ROT = 32
TQ = 512
LOG2E = 1.4426950408889634
MIB = 2**20


def dot_nt(a, b):
    return lax.dot_general(a, b, (((1,), (1,)), ((), ())), preferred_element_type=F32)


def dot_nn(a, b):
    return lax.dot_general(a, b, (((1,), (0,)), ((), ())), preferred_element_type=F32)


class Scratch:
    def __init__(self, names, refs):
        for name, ref in zip(names, refs):
            setattr(self, name, ref)


class Place:
    def __init__(self):
        f, s, t = (lax.axis_index(a) for a in ("fsdp", "sp", "tp"))
        self.f, self.s = f, s
        self.x, self.y, self.c, self.z = s % 4, (s // 4) * 2 + f // 2, f % 2, t
        self.a1 = self.x * (1 - self.c) + self.y * self.c
        self.a2 = self.y * (1 - self.c) + self.x * self.c

    def xy(self, d1, d2):
        p1, p2, c = (self.a1 + d1 + 4) % 4, (self.a2 + d2 + 4) % 4, self.c
        return p1 * (1 - c) + p2 * c, p2 * (1 - c) + p1 * c

    def dev(self, x, y, c, z):
        return ((y % 2) * 2 + c, (y // 2) * 4 + x, z)

    def peer(self, d1, d2):
        x, y = self.xy(d1, d2)
        return self.dev(x, y, self.c, self.z)

    def sibling(self):
        return self.dev(self.x, self.y, 1 - self.c, self.z)

    def blk(self, d1, d2):
        x, y = self.xy(d1, d2)
        return ((y % 2) * 2 + self.c) * 8 + (y // 2) * 4 + x

    def zpeer(self, d):
        return self.dev(self.x, self.y, self.c, (self.z + d + 4) % 4)

    def sp_peer(self, k):
        return (self.f, (self.s + k) % 8, self.z)


def barrier(devices):
    sem = pltpu.get_barrier_semaphore()
    for d in devices:
        pl.semaphore_signal(sem, inc=1, device_id=d, device_id_type=MESH)
    pl.semaphore_wait(sem, len(devices))


def remote(src, dst, send, recv, device):
    pltpu.make_async_remote_copy(
        src_ref=src, dst_ref=dst, send_sem=send, recv_sem=recv, device_id=device, device_id_type=MESH
    ).start()


def wait_bytes(ref, sem):
    pltpu.make_async_copy(ref, ref, sem).wait()


STEP = (0, -1, 1, 2)


class Gather:
    def __init__(self, p, shard, w, send, recv, local):
        self.p, self.shard, self.w, self.send, self.recv, self.local = p, shard, w, send, recv, local

    def push(self, b, sem, device, half=None, src=None):
        dst = self.w.at[b] if half is None else self.w.at[b, pl.ds(32 * half, 32)]
        remote(dst if src is None else src, dst, self.send, self.recv.at[sem], device)

    def arrive(self, b, sem):
        wait_bytes(self.w.at[b], self.recv.at[sem])

    def start(self):
        p, s = self.p, self.shard
        own = p.blk(0, 0)
        for sem, device in ((0, p.peer(1, 0)), (1, p.peer(-1, 0)), (3, p.peer(0, 1)), (7, p.peer(0, -1)), (15, p.sibling())):
            self.push(own, sem, device, src=s)
        pltpu.make_async_copy(s, self.w.at[own], self.local).start()

    def second(self, j):
        p = self.p
        b = p.blk(STEP[j], 0)
        self.push(b, 3 + j, p.peer(0, 1))
        self.push(b, 7 + j, p.peer(0, -1))
        self.push(b, 15, p.sibling())

    def first_low(self):
        p = self.p
        b = p.blk(-1, 0)
        self.arrive(b, 0)
        self.push(b, 2, p.peer(1, 0), half=0)
        self.second(1)

    def first_high(self):
        p = self.p
        b = p.blk(1, 0)
        self.arrive(b, 1)
        self.push(b, 2, p.peer(-1, 0), half=1)
        self.second(2)

    def first_far(self):
        self.arrive(self.p.blk(2, 0), 2)
        self.second(3)

    def low(self, j):
        p = self.p
        b = p.blk(STEP[j], -1)
        self.arrive(b, 3 + j)
        self.push(b, 11 + j, p.peer(0, 1), half=0)
        self.push(b, 15, p.sibling())

    def high(self, j):
        p = self.p
        b = p.blk(STEP[j], 1)
        self.arrive(b, 7 + j)
        self.push(b, 11 + j, p.peer(0, -1), half=1)
        self.push(b, 15, p.sibling())

    def far(self, j):
        b = self.p.blk(STEP[j], 2)
        self.arrive(b, 11 + j)
        self.push(b, 15, self.p.sibling())

    def end(self):
        wait_bytes(self.w.at[pl.ds(0, 16)], self.recv.at[15])
        own = self.p.blk(0, 0)
        pltpu.make_async_copy(self.shard, self.w.at[own], self.local).wait()

    def drain(self):
        wait_bytes(self.w.at[pl.ds(0, 31)], self.send)

    def ticks(self):
        part = functools.partial
        return [
            self.first_low, self.first_high, part(self.low, 0), part(self.high, 0), self.first_far,
            part(self.low, 1), part(self.high, 1), part(self.far, 0), part(self.low, 2), part(self.high, 2), part(self.far, 1),
            part(self.low, 3), part(self.high, 3), part(self.far, 2), part(self.far, 3), self.end,
        ]


class Ticks:
    def __init__(self):
        self.todo, self.now = [], 0.0

    def add(self, time, fn):
        self.todo.append((time, len(self.todo), fn))
        self.todo.sort(key=lambda e: e[:2])

    def series(self, first, step, fns):
        for k, fn in enumerate(fns):
            self.add(first + k * step, fn)

    def serve(self):
        while self.todo and self.todo[0][0] <= self.now:
            self.todo.pop(0)[2]()

    def step(self, us):
        self.now += us
        self.serve()

    def until_time(self, time):
        self.now = max(self.now, time)
        self.serve()

    def until(self, fn):
        for time, _, f in self.todo:
            if f == fn:
                self.now = max(self.now, time)
        self.serve()


ATT = dict(
    q=((2048, 64), BF), k=((2048, 64), BF), v=((2048, 64), BF), g=((2048, 64), BF),
    kt=((64, 2048), BF), vt=((80, 2048), BF), gt=((64, 2048), F32),
    dkv=((2048, 128), F32), mx=((8, TQ), F32), st=((4, TQ, TQ), F32), e=((4, TQ, TQ), BF),
    ot=((80, TQ), F32), dq=((64, TQ), F32), g2=((TQ, 64), BF),
)


def split_heads(recv, seq, b):
    @pl.loop(0, 8)
    def _(i):
        part = recv[i, pl.ds(seq * 256, 256), :]
        rows = pl.ds(i * 256, 256)
        q, k, v, g = (part[:, 64 * n : 64 * n + 64] for n in range(4))
        b.q[rows, :] = q
        b.k[rows, :] = k
        b.v[rows, :] = v
        b.g[rows, :] = g
        cols = pl.ds(pl.multiple_of(i * 256, 256), 256)
        b.kt[:, cols] = k.astype(F32).T.astype(BF)
        b.vt[0:64, cols] = v.astype(F32).T.astype(BF)
        b.gt[:, cols] = g.astype(F32).T

    b.vt[64:80, :] = jnp.ones((16, 2048), BF)
    b.dkv[...] = jnp.zeros(b.dkv.shape, F32)


def attend_block(qi, seq, b, send, ticks):
    scale = 0.125 * LOG2E
    qrows = slice(qi * TQ, (qi + 1) * TQ)
    q = b.q[qrows, :]
    b.mx[...] = jnp.full((8, TQ), -1e30, F32)
    for j in range(qi + 1):
        st = dot_nt(b.k[j * TQ : (j + 1) * TQ, :], q)
        if j == qi:
            key = lax.broadcasted_iota(jnp.int32, (TQ, TQ), 0)
            query = lax.broadcasted_iota(jnp.int32, (TQ, TQ), 1)
            st = jnp.where(key <= query, st, -1e30)
        b.st[j] = st
        b.mx[...] = jnp.maximum(b.mx[...], jnp.max(st.reshape(TQ // 8, 8, TQ), axis=0))
        ticks.step(0.45)
    top = jnp.max(b.mx[...], axis=0, keepdims=True) * scale
    b.ot[...] = jnp.zeros(b.ot.shape, F32)
    for j in range(qi + 1):
        e = jnp.exp2(b.st[j] * scale - top).astype(BF)
        b.e[j] = e
        b.ot[...] += dot_nn(b.vt[:, j * TQ : (j + 1) * TQ], e)
        ticks.step(0.45)
    inv = 1.0 / b.ot[64:65, :]
    out = b.ot[0:64, :] * inv
    gt = b.gt[:, qrows] * inv
    inner = jnp.sum(out * gt, axis=0, keepdims=True)
    b.g2[...] = gt.T.astype(BF)
    b.dq[...] = jnp.zeros(b.dq.shape, F32)
    for j in range(qi + 1):
        rows = slice(j * TQ, (j + 1) * TQ)
        g2 = b.g2[...]
        dp = dot_nt(b.v[rows, :], g2)
        e = b.e[j]
        ds = (e.astype(F32) * (dp - inner)).astype(BF)
        b.dkv[rows, 0:64] += dot_nn(ds, b.q[qrows, :])
        b.dkv[rows, 64:128] += dot_nn(e, g2)
        b.dq[...] += dot_nn(b.kt[:, j * TQ : (j + 1) * TQ], ds)
        ticks.step(0.9)
    both = jnp.concatenate([out, b.dq[...] * 0.125], axis=0).T.astype(BF)
    for h in range(2):
        send[qi * 2 + h, seq * 256 : (seq + 1) * 256, 0:128] = both[h * 256 : (h + 1) * 256]


def finish_heads(seq, b, send):
    @pl.loop(0, 8)
    def _(i):
        t = b.dkv[pl.ds(i * 256, 256), :]
        lane = lax.broadcasted_iota(jnp.int32, t.shape, 1)
        send[i, pl.ds(seq * 256, 256), 128:256] = (t * jnp.where(lane < 64, 0.125, 1.0)).astype(BF)


def turn(a, cos, low, high):
    return a * cos + pltpu.roll(a, 112, 1) * low + pltpu.roll(a, 16, 1) * high


FAR_FIRST = (2, 1, -1, 0)


class Scatter:
    def __init__(self, p, product, r, sbuf, rest, ssend, srecv, send, recv):
        self.p, self.product, self.r, self.sbuf = p, product, r, sbuf
        self.half, self.full = (lambda j, h: rest(j, 32 * h, 32)), (lambda j, h: rest(4 + 2 * j + h, 0, 64))
        self.half1, self.full1 = (lambda h: rest(12, 32 * h, 32)), (lambda h: rest(13 + h, 0, 64))
        self.ssend, self.srecv, self.send, self.recv = ssend, srecv, send, recv

    def rb(self, d1, d2):
        x, y = self.p.xy(d1, d2)
        return ((y % 2) * 2 + y // 2) * 4 + x

    def hand_over(self, n):
        low = (self.p.y + n) % 2
        blocks = pl.ds(low * 8, 8)

        def store(cols, value):
            self.sbuf[blocks, :, cols] = value.astype(BF).reshape(8, 64, value.shape[1])

        self.product(low, 1 - self.p.c, store)
        remote(self.sbuf.at[blocks], self.r.at[blocks], self.ssend, self.srecv.at[n], self.p.sibling())

    def handed_over(self):
        wait_bytes(self.sbuf, self.ssend)

    def own_rows(self, n):
        low = (self.p.y + n) % 2
        blocks = pl.ds(low * 8, 8)
        wait_bytes(self.r.at[blocks], self.srecv.at[n])

        def store(cols, value):
            total = value.reshape(8, 64, value.shape[1]) + self.r[blocks, :, cols].astype(F32)
            self.r[blocks, :, cols] = total.astype(BF)

        self.product(low, self.p.c, store)

    def add(self, dst, src):
        dst[...] = (dst[...].astype(F32) + src[...].astype(F32)).astype(BF)

    def rows(self, d1, d2, h):
        return self.r.at[self.rb(d1, d2), pl.ds(32 * h, 32)]

    def far(self, j):
        p, d = self.p, FAR_FIRST[j]
        for h, to in ((0, 1), (1, -1)):
            remote(self.rows(d, 2, h), self.half(j, h), self.send, self.recv.at[2 * j + h], p.peer(0, to))

    def near(self, j):
        p, d = self.p, FAR_FIRST[j]
        for h, to in ((0, 1), (1, -1)):
            wait_bytes(self.half(j, h), self.recv.at[2 * j + h])
            self.add(self.rows(d, to, h), self.half(j, h))
            remote(self.r.at[self.rb(d, to)], self.full(j, h), self.send, self.recv.at[8 + 2 * j + h], p.peer(0, to))

    def sum(self, j):
        for h in range(2):
            wait_bytes(self.full(j, h), self.recv.at[8 + 2 * j + h])
        dst = self.r.at[self.rb(FAR_FIRST[j], 0)]
        dst[...] = (dst[...].astype(F32) + self.full(j, 0)[...].astype(F32) + self.full(j, 1)[...].astype(F32)).astype(BF)

    def far1(self):
        for h, to in ((0, 1), (1, -1)):
            remote(self.rows(2, 0, h), self.half1(h), self.send, self.recv.at[16 + h], self.p.peer(to, 0))

    def near1(self):
        for h, to in ((0, 1), (1, -1)):
            wait_bytes(self.half1(h), self.recv.at[16 + h])
            self.add(self.rows(to, 0, h), self.half1(h))
            remote(self.r.at[self.rb(to, 0)], self.full1(h), self.send, self.recv.at[18 + h], self.p.peer(to, 0))

    def sum1(self, out):
        for h in range(2):
            wait_bytes(self.full1(h), self.recv.at[18 + h])
        out[...] = self.r[self.rb(0, 0)].astype(F32) + self.full1(0)[...].astype(F32) + self.full1(1)[...].astype(F32)

    def drain(self):
        wait_bytes(self.r.at[pl.ds(0, 15)], self.send)


class Depth:
    def __init__(self, p, a, half, full, rsend, gsend, recv, spare, one):
        self.p, self.a, self.half, self.full, self.spare, self.one = p, a, half, full, spare, one
        self.rsend, self.gsend, self.recv = rsend, gsend, recv

    def rows(self, ref, d, h=None):
        z = (self.p.z + d + 4) % 4
        return ref.at[pl.ds(z * 128, 128)] if h is None else ref.at[pl.ds(z * 128 + 64 * h, 64)]

    def far(self):
        for h, to in ((0, 1), (1, -1)):
            remote(self.rows(self.a, 2, h), self.half.at[h], self.rsend, self.recv.at[h], self.p.zpeer(to))

    def near(self):
        for h, to in ((0, 1), (1, -1)):
            wait_bytes(self.half.at[h], self.recv.at[h])
            dst = self.rows(self.a, to, h)
            dst[...] = (dst[...].astype(F32) + self.half[h].astype(F32)).astype(BF)
            remote(self.rows(self.a, to), self.full.at[h], self.rsend, self.recv.at[2 + h], self.p.zpeer(to))

    def release(self):
        wait_bytes(self.a.at[pl.ds(0, 384)], self.rsend)
        for to in (1, -1):
            pl.semaphore_signal(self.spare, inc=self.one, device_id=self.p.zpeer(to), device_id_type=MESH)

    def arrived(self):
        for h in range(2):
            wait_bytes(self.full.at[h], self.recv.at[2 + h])

    def total(self, r):
        own = self.a[pl.ds(self.p.z * 128 + r, 32), :].astype(F32)
        return own + self.full[0, pl.ds(r, 32), :].astype(F32) + self.full[1, pl.ds(r, 32), :].astype(F32)

    def give(self):
        pl.semaphore_wait(self.spare, self.one * 2)
        src = self.rows(self.a, 0)
        for h, to in ((0, 1), (1, -1)):
            remote(src, src, self.gsend, self.recv.at[4 + h], self.p.zpeer(to))

    def give_on(self):
        for h, to in ((0, 1), (1, -1)):
            wait_bytes(self.rows(self.a, -to), self.recv.at[4 + h])
            src = self.rows(self.a, -to, h)
            remote(src, src, self.gsend, self.recv.at[6], self.p.zpeer(to))

    def given(self):
        wait_bytes(self.rows(self.a, 2), self.recv.at[6])

    def drain(self):
        wait_bytes(self.a.at[pl.ds(0, 384)], self.gsend)


K1 = dict(
    wa=((32, 64, 2048), BF), wb=((32, 64, 2048), BF), wc=((32, 64, 2048), BF),
    hid=((512, 2048), BF), gv=((512, 2048), BF), act=((512, 2048), BF), din=((512, 2048), BF),
    hs=((8, 512, 256), BF), hr=((8, 512, 256), BF), br=((8, 512, 256), BF), gp=((512, 2048), BF),
    dproj=((512, 1536), BF), att=((512, 512), BF), sums=((8, 2048), F32), sa=((64, 2048), BF),
    prm=((8, 2048), F32), bq=((3, 512), F32), cos=((256, 128), F32), low=((256, 128), F32), high=((256, 128), F32),
)
LATE = dict(
    rc=((47, 64, 2048), BF), zh=((2, 2, 64, 2048), BF), zf=((2, 2, 128, 2048), BF),
    res=((64, 2048), F32), vec=((5, 8, 2048), F32), vin=((10, 8, 2048), F32),
)

EARLY_NEAR = False
SERVE_A = (6.0, 1.7)
START_B = 14.0
SERVE_B = (40.0, 2.0)
START_C = 40.0
SERVE_C = (58.0, 2.5)
HEADS_IN = 40.0


def block_kernel(
    x_hbm, g_hbm, wq, wd, sb, sc, r_gain, r_shift, r_bd, r_b2, r_b1, r_bqkv,
    o_mixed, o_tok, o_res, o_vec, o_ht, o_gt, *refs,
):
    m = Scratch(K1, refs[: len(K1)])
    (
        wsend, wrecv, wlocal, asend, arecv, local, lout, ssend, srecv, send, recv, zrs, zgs, zrecv, vsend, vrecv, here, free, spare,
    ) = refs[len(K1) :]
    p = Place()
    pieces = [pltpu.make_async_copy(wq.at[n], m.sa.at[:, n * 512 : n * 512 + 512], local.at[0]) for n in range(3)]
    pieces.append(pltpu.make_async_copy(wd, m.sa.at[:, 1536:2048], local.at[0]))
    for c in pieces:
        c.start()
    shard = pltpu.make_async_copy(m.sa, m.sa, local.at[0])
    xs = [p.dev((p.x + k) % 4, p.y, p.c, p.z) for k in (1, 2, 3)]
    ys = [p.dev(p.x, (p.y + k) % 4, p.c, p.z) for k in (1, 2, 3)]
    zs = [p.zpeer(k) for k in (1, 2, 3)]
    far = [p.dev((p.x + k) % 4, (p.y + 2) % 4, p.c, p.z) for k in (1, 2, 3)]
    barrier(xs + ys + zs + far + [p.sibling()])
    near = [xs[0], xs[2], ys[0], ys[2], zs[0], zs[2], p.sibling()]

    one = p.z * 0 + 1
    seven = one * 7

    def say(sem):
        for d in near:
            pl.semaphore_signal(sem, inc=one, device_id=d, device_id_type=MESH)

    ga, gb, gc = (
        Gather(p, s, w, wsend.at[i], wrecv.at[i], wlocal.at[i]) for i, (s, w) in enumerate(((m.sa, m.wa), (sb, m.wb), (sc, m.wc)))
    )
    for row, src in ((0, r_gain), (1, r_shift), (2, r_bd), (3, r_b2), (4, r_b1)):
        part = src[...].astype(F32)
        for n in range(16):
            m.prm[row : row + 1, n * 128 : n * 128 + 128] = part[n : n + 1]
    m.bq[...] = r_bqkv[...].astype(F32)
    prm, bqkv = m.prm, m.bq
    shard.wait()
    ga.start()
    load_x = pltpu.make_async_copy(x_hbm, m.act, local.at[0])
    load_g = pltpu.make_async_copy(g_hbm, m.gv, local.at[1])
    load_x.start()
    load_g.start()
    ticks = Ticks()
    ticks.series(*SERVE_A, ga.ticks())
    ticks.add(START_B, gb.start)
    ticks.series(*SERVE_B, gb.ticks())
    ticks.add(START_C, gc.start)
    ticks.series(*SERVE_C, gc.ticks())

    lane = lax.broadcasted_iota(jnp.int32, (256, 128), 1) % 64
    place = (p.s * 256 + lax.broadcasted_iota(jnp.int32, (256, 128), 0)).astype(F32)
    angle = place * jnp.exp((lane % 16).astype(F32) * (-2.0 * math.log(10000.0) / ROT))
    sine = jnp.sin(angle)
    m.cos[...] = jnp.where(lane < 32, jnp.cos(angle), 1.0)
    m.low[...] = jnp.where(lane < 16, -sine, 0.0)
    m.high[...] = jnp.where((lane >= 16) & (lane < 32), sine, 0.0)
    cos, low, high = m.cos, m.low, m.high
    gain, shift, bfc1 = prm.at[0:1], prm.at[1:2], prm.at[4:5]
    load_x.wait()

    def norm_rows(n):
        @pl.loop(0, 4)
        def _(r):
            rows = pl.ds(n * 128 + r * 32, 32)
            x = m.act[rows, :].astype(F32)
            cent = x - jnp.mean(x, axis=-1, keepdims=True)
            inv = lax.rsqrt(jnp.mean(cent * cent, axis=-1, keepdims=True) + 1e-05)
            m.hid[rows, :] = (cent * inv * gain[...] + shift[...]).astype(BF)

    for n in range(4):
        norm_rows(n)
        ticks.step(0.9)
    outs = []

    def put(src, dst):
        c = pltpu.make_async_copy(src, dst, lout.at[len(outs)])
        c.start()
        outs.append(c)

    load_g.wait()

    def flip(src, dst, n):
        at, half = n // 2, n % 2
        dst[at * 2 + half] = src[half * 256 : half * 256 + 256, at * 512 : at * 512 + 512].astype(F32).T.astype(BF)

    for n in range(8):
        flip(m.gv, m.hs, n)
        ticks.step(0.4)
    put(m.hs, o_gt)
    for n in range(8):
        flip(m.hid, m.br, n)
        ticks.step(0.4)
    put(m.br, o_ht)

    @pl.loop(0, 8)
    def _(n):
        cols = pl.ds(pl.multiple_of(n * 256, 256), 256)
        m.sums[2:3, cols] = jnp.sum(m.gv[:, cols].astype(F32), axis=0, keepdims=True)

    ticks.until(ga.end)

    outs[0].wait()
    outs[1].wait()

    for part in range(4):
        for t in range(2):
            col = part * 512 + t * 256
            lhs = m.gv if part == 3 else m.hid
            acc = dot_nn(lhs[...], m.wa[:, :, col : col + 256].reshape(2048, 256))
            if part < 3:
                acc = acc + bqkv[part : part + 1, t * 256 : t * 256 + 256]
            for sq in range(2):
                for lh in range(2):
                    a = acc[sq * 256 : (sq + 1) * 256, lh * 128 : (lh + 1) * 128]
                    if part < 2:
                        a = turn(a, cos[...], low[...], high[...])
                    a = a.astype(BF)
                    for e in range(2):
                        m.hs[t * 4 + lh * 2 + e, sq * 256 : (sq + 1) * 256, part * 64 : part * 64 + 64] = a[:, e * 64 : e * 64 + 64]
            ticks.step(0.75)

    def exchange(dst, recv, seq, base):
        rows = pl.ds(seq * 256, 256)
        for k in range(1, 8):
            to = (p.s + k) % 8
            remote(m.hs.at[to, rows], dst.at[p.s, rows], asend.at[base], recv, p.sp_peer(k))
        pltpu.make_async_copy(m.hs.at[p.s, rows], dst.at[p.s, rows], local.at[2 + base]).start()

    def exchanged(dst, recv, seq, base):
        rows = pl.ds(seq * 256, 256)
        wait_bytes(dst.at[pl.ds(0, 7), rows], recv)
        pltpu.make_async_copy(m.hs.at[p.s, rows], dst.at[p.s, rows], local.at[2 + base]).wait()

    def sent(base):
        wait_bytes(m.hs.at[pl.ds(0, 7), pl.ds(0, 256)], asend.at[base])

    for seq in range(2):
        exchange(m.hr, arecv.at[seq], seq, seq)
    ticks.step(1.0)
    ticks.until_time(HEADS_IN)


    def heads(*scratch):
        b = Scratch(ATT, scratch)
        for seq in range(2):
            exchanged(m.hr, arecv.at[seq], seq, seq)
            split_heads(m.hr, seq, b)
            ticks.step(1.5)
            if seq == 0:
                sent(0)
                sent(1)
            for qi in range(4):
                attend_block(qi, seq, b, m.hs, ticks)
            finish_heads(seq, b, m.hs)
            ticks.step(0.7)
            exchange(m.br, arecv.at[2 + seq], seq, 2 + seq)

    pl.run_scoped(heads, *[pltpu.VMEM(*v) for v in ATT.values()])
    load_gt = pltpu.make_async_copy(o_gt, m.hr, local.at[0])
    load_gt.start()

    def hidden_units(n):
        cols = slice(n * 256, n * 256 + 256)
        u = dot_nn(m.hid[...], m.wb[:, :, cols].reshape(2048, 256)) + bfc1[:, cols]
        k = math.sqrt(2.0 / math.pi)
        sq = u * u
        th = jnp.tanh(u * (k + (k * 0.044715) * sq))
        half = 0.5 + 0.5 * th
        m.act[:, cols] = (u * half).astype(BF)
        m.gp[:, cols] = (half + (0.5 * u) * (1.0 - th * th) * (k + (3.0 * k * 0.044715) * sq)).astype(BF)

    ticks.until(gb.end)
    for n in range(8):
        hidden_units(n)
        ticks.step(0.9)

    def late(*scratch):
        b = Scratch(LATE, scratch)
        say(here)
        finish(b)

    def finish(b):
        def product(pairs):
            def run(low, cc, store):
                def tile(left, right, col, dst):
                    at = (low * 2 + cc) * 2
                    store(dst, dot_nn(left[at], right[0:256, col]) + dot_nn(left[at + 1], right[256:512, col]))

                for left, right, start, count in pairs:

                    @pl.loop(0, count)
                    def _(t):
                        tile(left, right, pl.ds(pl.multiple_of(t * 512, 512), 512), pl.ds(pl.multiple_of(start + t * 512, 512), 512))

            return run

        pairs = ([(m.hr, m.act, 0, 4)], [(m.hs, m.din, 0, 4)], [(m.hs, m.dproj, 0, 3), (m.hr, m.att, 1536, 1)])

        def rows_of(ref, base):
            return lambda n, start, count: ref.at[base + n, pl.ds(start, count)]

        spaces = (
            (b.rc.at[pl.ds(0, 16)], b.rc.at[pl.ds(16, 16)], rows_of(b.rc, 32)),
            (m.wa.at[pl.ds(0, 16)], m.wa.at[pl.ds(16, 16)], rows_of(m.wb, 0)),
            (m.wc.at[pl.ds(0, 16)], m.wc.at[pl.ds(16, 16)], rows_of(m.wb, 15)),
        )
        sc = [Scatter(p, product(pairs[i]), *spaces[i], ssend.at[i], srecv.at[i], send.at[i], recv.at[i]) for i in range(3)]
        zn, zm = (Depth(p, a, b.zh.at[i], b.zf.at[i], zrs.at[i], zgs.at[i], zrecv.at[i], spare.at[i], one) for i, a in enumerate((m.hid, m.gv)))
        v = b.vec.at[0]
        gain, bout = prm.at[0:1], prm[2:3, :] + prm[3:4, :]

        def norm_back(i):
            r = i * 32
            x32 = m.act[pl.ds(r, 32), :].astype(F32)
            cent = x32 - jnp.mean(x32, axis=-1, keepdims=True)
            inv = lax.rsqrt(jnp.mean(cent * cent, axis=-1, keepdims=True) + 1e-05)
            xn = cent * inv
            gn = zn.total(r)
            v[0:1, :] += jnp.sum(gn * xn, axis=0, keepdims=True)
            v[1:2, :] += jnp.sum(gn, axis=0, keepdims=True)
            gn = gn * gain[...]
            gx = inv * (gn - jnp.mean(gn, axis=-1, keepdims=True) - xn * jnp.mean(gn * xn, axis=-1, keepdims=True))
            m.hid[pl.ds(p.z * 128 + r, 32), :] = (m.act[pl.ds(128 + r, 32), :].astype(F32) + gx).astype(BF)

        def vsends(stage, peers, base):
            for i, d in enumerate(peers):
                remote(b.vec.at[stage], b.vin.at[base + i], vsend, vrecv.at[base + i], d)

        def vsum(stage, count, base, rows):
            total = b.vec[stage]
            for i in range(count):
                wait_bytes(b.vin.at[base + i], vrecv.at[base + i])
                part = b.vin[base + i]
                if rows < 8:
                    part = jnp.where(lax.broadcasted_iota(jnp.int32, part.shape, 0) < rows, part, 0.0)
                total = total + part
            b.vec[stage + 1] = total

        def hand(i, n):
            sc[i].hand_over(n)

        def own(i, n):
            sc[i].own_rows(n)
            for j in ((0, 3), (1, 2))[n]:
                sc[i].far(j)

        def last(i):
            if i > 0:
                wait_bytes(b.res, local.at[0])
            sc[i].sum1(b.res)
            pltpu.make_async_copy(b.res, o_res.at[i], local.at[0]).start()

        v[...] = jnp.zeros((8, 2048), F32)
        load_gt.wait()
        pl.semaphore_wait(here, seven)
        for n in range(2):
            hand(0, n)
            ticks.step(1.5)
        for seq in range(2):
            exchanged(m.br, arecv.at[2 + seq], seq, 2 + seq)
        sent(2)
        sent(3)
        load_ht = pltpu.make_async_copy(o_ht, m.hs, local.at[1])
        load_ht.start()

        for hp in range(4):
            pair = [m.br[2 * hp + e] for e in range(2)]
            for n in range(4):
                a = jnp.concatenate([pair[e][:, n * 64 : n * 64 + 64] for e in range(2)], axis=1)
                cols = slice(hp * 128, hp * 128 + 128)
                if n == 0:
                    m.att[:, cols] = a
                    continue
                if n < 3:
                    a = a.astype(F32)
                    a = jnp.concatenate(
                        [turn(a[sq * 256 : sq * 256 + 256], cos[...], -low[...], -high[...]) for sq in range(2)], axis=0
                    ).astype(BF)
                cols = slice((n - 1) * 512 + hp * 128, (n - 1) * 512 + hp * 128 + 128)
                m.dproj[:, cols] = a
                m.sums[1:2, cols] = jnp.sum(a.astype(F32), axis=0, keepdims=True)
            ticks.step(0.6)
        for t in range(4):
            rows, cols = slice(t * 8, t * 8 + 8), slice(t * 512, t * 512 + 512)
            m.hid[:, cols] = dot_nt(m.dproj[...], m.wa[rows, :, 0:1536].reshape(512, 1536)).astype(BF)
            ticks.step(0.9)
        for t in range(4):
            rows = slice(t * 8, t * 8 + 8)
            part = dot_nt(m.att[...], m.wa[rows, :, 1536:2048].reshape(512, 512)).astype(BF)
            for e in range(2):
                m.br[2 * t + e] = part[:, e * 256 : e * 256 + 256]
            ticks.step(0.35)
        ga.drain()
        say(free.at[0])
        for n in range(2):
            own(0, n)
            ticks.step(1.8)
        if EARLY_NEAR:
            for j in range(4):
                sc[0].near(j)
        ticks.until(gc.end)
        for n in range(8):
            if not EARLY_NEAR and n % 2 == 0:
                sc[0].near(n // 2)
            cols = slice(n * 256, n * 256 + 256)
            ga_ = dot_nn(m.gv[...], m.wc[:, :, cols].reshape(2048, 256))
            d = (ga_ * m.gp[:, cols].astype(F32)).astype(BF)
            m.din[:, cols] = d
            m.sums[0:1, cols] = jnp.sum(d.astype(F32), axis=0, keepdims=True)
        @pl.loop(0, 4)
        def _(t):
            rows = pl.ds(t * 8, 8)
            cols = pl.ds(pl.multiple_of(t * 512, 512), 512)
            norm = m.hid[:, cols].astype(F32) + dot_nt(m.din[...], m.wb[rows].reshape(512, 2048))
            m.hid[:, cols] = norm.astype(BF)

        zn.far()
        gb.drain()
        say(free.at[1])
        load_ht.wait()
        pl.semaphore_wait(free.at[0], seven)
        for n in range(2):
            hand(1, n)

        @pl.loop(0, 4)
        def _(t):
            rows = pl.ds(t * 8, 8)
            cols = pl.ds(pl.multiple_of(t * 512, 512), 512)
            part = jnp.concatenate([m.br[2 * t], m.br[2 * t + 1]], axis=1)
            mixed = part.astype(F32) + dot_nt(m.act[...], m.wc[rows].reshape(512, 2048))
            m.gv[:, cols] = mixed.astype(BF)

        zm.far()
        zrow = pl.ds(p.z * 128, 128)
        halves = (m.act.at[pl.ds(0, 128)], m.act.at[pl.ds(128, 128)])
        loads = [pltpu.make_async_copy(s.at[zrow], d, local.at[6 + i]) for i, (s, d) in enumerate(zip((x_hbm, g_hbm), halves))]
        for c in loads:
            c.start()
        gc.drain()
        say(free.at[2])
        zn.near()
        pl.semaphore_wait(free.at[1], seven)
        own(1, 0)
        sc[0].sum(0)
        sc[0].far1()
        own(1, 1)
        zm.near()
        sc[0].sum(1)
        sc[0].sum(2)
        sc[0].near1()
        pl.semaphore_wait(free.at[2], seven)
        for n in range(2):
            hand(2, n)
        for c in loads:
            c.wait()
        zn.arrived()
        zn.release()

        @pl.loop(0, 4)
        def _(i):
            norm_back(i)

        zn.give()
        v[2:3, :] = m.sums[2:3, :]
        v[3:4, :] = m.sums[0:1, :]
        v[4:5, :] = m.sums[1:2, :]
        vsends(0, zs, 0)
        sc[1].near(0)
        sc[1].near(1)
        sc[1].near(2)
        sc[1].near(3)
        own(2, 0)
        own(2, 1)
        zm.arrived()
        zm.release()

        @pl.loop(0, 4)
        def _(i):
            r = i * 32
            total = zm.total(r) + m.act[pl.ds(r, 32), :].astype(F32) + bout
            m.gv[pl.ds(p.z * 128 + r, 32), :] = total.astype(BF)

        zm.give()
        sc[0].sum(3)
        last(0)
        sc[1].sum(0)
        sc[1].far1()
        vsum(0, 3, 0, 2)
        vsends(1, ys, 3)
        sc[1].sum(1)
        sc[1].sum(2)
        sc[1].near1()
        zn.give_on()
        sc[2].near(0)
        sc[2].near(1)
        sc[2].near(2)
        sc[2].near(3)
        vsum(1, 3, 3, 8)
        vsends(2, xs, 6)
        sc[1].sum(3)
        sc[2].sum(0)
        sc[2].far1()
        last(1)
        zm.give_on()
        sc[2].sum(1)
        sc[2].sum(2)
        sc[2].near1()
        vsum(2, 3, 6, 8)
        vsends(3, [p.sibling()], 9)
        zn.given()
        put(m.hid, o_tok)
        sc[2].sum(3)
        zm.given()
        put(m.gv, o_mixed)
        vsum(3, 1, 9, 8)
        put(b.vec.at[4], o_vec)
        last(2)
        wait_bytes(b.res, local.at[0])
        for s in sc:
            s.drain()
            s.handed_over()
        zn.drain()
        zm.drain()
        wait_bytes(b.vin, vsend)
        for c in outs[2:]:
            c.wait()

    pl.run_scoped(late, *[pltpu.VMEM(*v) for v in LATE.values()])


def run_block(x, g, wq, wd, sb, sc, *small):
    hbm = pl.BlockSpec(memory_space=pl.ANY)
    vmem = pl.BlockSpec(memory_space=pltpu.VMEM)
    full = jax.ShapeDtypeStruct((512, 2048), BF)
    flipped = jax.ShapeDtypeStruct((8, 512, 256), BF)
    dma, plain = pltpu.SemaphoreType.DMA, pltpu.SemaphoreType.REGULAR
    return pl.pallas_call(
        block_kernel,
        out_shape=[full, full, jax.ShapeDtypeStruct((3, 64, 2048), F32), jax.ShapeDtypeStruct((8, 2048), F32), flipped, flipped],
        in_specs=[hbm] * 6 + [vmem] * 6,
        out_specs=[hbm] * 6,
        scratch_shapes=[pltpu.VMEM(*v) for v in K1.values()]
        + [dma((3,)), dma((3, 16)), dma((3,)), dma((4,)), dma((4,)), dma((8,)), dma((8,))]
        + [dma((3,)), dma((3, 2)), dma((3,)), dma((3, 20)), dma((2,)), dma((2,)), dma((2, 7)), dma(()), dma((10,)), plain, plain((3,)), plain((2,))],
        compiler_params=pltpu.CompilerParams(collective_id=0, has_side_effects=True, vmem_limit_bytes=63 * MIB),
        cost_estimate=pl.CostEstimate(flops=43 * 10**9, bytes_accessed=30 * 10**6, transcendentals=10**7),
    )(x, g, wq, wd, sb, sc, *small)


def place_kernel(mixed, tok, res, vec, o_mixed, o_tok, gq, gd, g1, g2, gain, shift, bq, bo, b1, bo2, *scratch):
    a, b, r, come, go = scratch
    loads = [pltpu.make_async_copy(s, d, come.at[i]) for i, (s, d) in enumerate(((mixed, a), (tok, b), (res, r)))]
    for c in loads:
        c.start()
    for row, out in ((0, gain), (1, shift), (2, bo), (2, bo2), (3, b1)):
        out[...] = vec[row : row + 1, :]
    for n in range(3):
        bq[n : n + 1, :] = vec[4:5, n * 512 : n * 512 + 512]
    moves = [(a, o_mixed, 0), (b, o_tok, 1), (r.at[1], g1, 2), (r.at[0], g2, 2), (r.at[2, :, pl.ds(1536, 512)], gd, 2)]
    moves += [(r.at[2, :, pl.ds(n * 512, 512)], gq.at[n], 2) for n in range(3)]
    copies = [pltpu.make_async_copy(s, d, go.at[i]) for i, (s, d, _) in enumerate(moves)]
    for i, c in enumerate(loads):
        c.wait()
        for move, copy in zip(moves, copies):
            if move[2] == i:
                copy.start()
    for c in copies:
        c.wait()


def place_outputs(mixed, tok, res, vec):
    hbm = pl.BlockSpec(memory_space=pl.ANY)
    vmem = pl.BlockSpec(memory_space=pltpu.VMEM)
    full = jax.ShapeDtypeStruct((512, 2048), BF)

    def f32(*shape):
        return jax.ShapeDtypeStruct(shape, F32)

    row = f32(1, 2048)
    dma = pltpu.SemaphoreType.DMA
    return pl.pallas_call(
        place_kernel,
        out_shape=[full, full, f32(3, 64, 512), f32(64, 512), f32(64, 2048), f32(64, 2048), row, row, f32(3, 512), row, row, row],
        in_specs=[hbm] * 3 + [vmem],
        out_specs=[hbm] * 6 + [vmem] * 6,
        scratch_shapes=[pltpu.VMEM((512, 2048), BF)] * 2 + [pltpu.VMEM((3, 64, 2048), F32), dma((3,)), dma((8,))],
        compiler_params=pltpu.CompilerParams(vmem_limit_bytes=60 * MIB),
    )(mixed, tok, res, vec)


def body(tokens, ln_gain, ln_bias, w_qkv, b_qkv, w_dense, b_dense, w_fc1, b_fc1, w_fc2, b_fc2, cotangent):
    width = tokens.shape[2]
    x = tokens.reshape(-1, width)
    g = cotangent.reshape(-1, width)
    small = (ln_gain, ln_bias, b_dense, b_fc2, b_fc1)
    mixed_out, grad_tokens, res, vec, _, _ = run_block(
        x, g, w_qkv.transpose(1, 0, 2), w_dense.T, w_fc1, w_fc2.T, *[v.reshape(16, 128) for v in small], b_qkv
    )
    mixed_out, grad_tokens, gq, gd, g1, g2, gain, shift, bq, bo, b1, bo2 = place_outputs(mixed_out, grad_tokens, res, vec)
    return (
        mixed_out.reshape(tokens.shape), grad_tokens.reshape(tokens.shape), gain[0], shift[0], gq.transpose(1, 0, 2), bq, gd.T,
        bo[0], g1, b1[0], g2.T, bo2[0],
    )


def solution(mesh):
    both = ("fsdp", "sp")
    act = P("fsdp", "sp", None)
    in_specs = (
        act, P(), P(), P(both, None, "tp"), P(None, "tp"), P("tp", both), P(), P(both, "tp"), P("tp"), P("tp", both), P(), act,
    )
    out_specs = (
        act, act, P(), P(), P(both, None, "tp"), P(None, "tp"), P("tp", both), P(), P(both, "tp"), P("tp"), P("tp", both), P(),
    )
    return jax.shard_map(body, mesh=mesh, in_specs=in_specs, out_specs=out_specs, check_vma=False)
```
